32 devices in a mesh: exp: 2 (over x), row: 16 (over z, y, core).
Axes of the slice: x: 2, y: 2, z: 4, core: 2. Of those that a mesh axis runs over, the one named last changes fastest.
Arguments:
- brightness: float32 [3072], P(('exp', 'row')), parts along dimension 0, may hold values from 0.5 to 4
- subpixel: float32 [2, 3072], P(None, ('exp', 'row')), parts along dimension 1, may hold values from 0 to 1
- profile_width: float32 [3072], P(('exp', 'row')), parts along dimension 0, may hold values from 0.4 to 2.5
- psf_coef: bfloat16 [21, 3072], P(None, ('exp', 'row')), parts along dimension 1, may hold values from -6 to 6
- row_offset: int32 [3072], P(('exp', 'row')), parts along dimension 0, may hold values from -64 to 64
- column_offset: int32 [3072], P(('exp', 'row')), parts along dimension 0, may hold values from 0 to 3968
- send_list: int32 [32, 16, 10], P(('exp', 'row')), parts along dimension 0, may hold values from 0 to 95, as said below
- send_count: int32 [32, 16], P(('exp', 'row')), parts along dimension 0, may hold values from 0 to 10, as said below
- psf_basis: bfloat16 [21, 128, 128], replicated, may hold values from -1.25 to 1.25
- vertical_kernel: float32 [9], replicated, may hold values from 0.02 to 0.2
- horizontal_kernel: float32 [9], replicated, may hold values from 0.02 to 0.2
Outputs:
- sensor_image: float32 [4096, 4096], P(('exp', 'row')), parts along dimension 0
The draws below stay inside these ranges and needn't reach their ends.
There are 2 independent parts, one for each index of `exp`. The reference program is written for one: setup_inputs(seed, part) draws one part's arguments, and reference() takes and returns one part's arrays. A program takes and returns all parts, laid end to end along the dimension named above; an argument that names none is the same for every part. Nothing has to cross between parts.
Inputs may be any that keep to these rules, and one draw needn't show every extreme that they name: `send_count`: entry [d, t] counts the objects of sky cell d drawn on sensor row block t. In every draw one block receives exactly 10 from every cell; each cell's counts sum to at most 96. `send_list`: indices into the sending cell's 96 objects; the live entries of one cell are distinct over all its lists; the other entries are arbitrary.
All inputs are finite; a program needn't handle non-finite values.
Results may differ from the reference program's by a relative error of at most 0.005.
Values may be sent and summed in bfloat16 or wider, within the bound.
No kernel may reach another device: no remote copies, remote signals or barrier semaphores. Data moves between devices by JAX's collectives and lax.ppermute only.
A program may use at most 128 MiB of HBM per device.

```python
import math
import jax
import jax.numpy as jnp
from jax import lax

STAMP = 128
PSF_TERMS = 21
SENSOR_COLS = 4096
H_DEV = 128
OBJ_DEV = 96
CELLS = 16
CAP = 10
OBJ_TOTAL = 1536
ROWS_TOTAL = 2048
TAPS = 9


def cell_loads(key):
    busiest = jax.random.randint(jax.random.fold_in(key, 101), (), 0, CELLS)
    lighter = jax.random.randint(jax.random.fold_in(key, 102), (CELLS, CELLS), 0, CAP // 2 + 1)
    targets = jnp.arange(CELLS, dtype=jnp.int32)
    return jnp.where(targets[None, :] == busiest, CAP, lighter).astype(jnp.int32)


def draw_send_count(key, part):
    return cell_loads(key)


def draw_send_list(key, part):
    loads = cell_loads(key)
    key = jax.random.fold_in(key, 7)
    starts = jnp.cumsum(loads, axis=1) - loads
    slot_ids = jnp.arange(CAP, dtype=jnp.int32)
    ranking = starts[:, :, None] + slot_ids[None, None, :]
    rotation = OBJ_DEV - 1 - jax.random.randint(key, (CELLS, 1, 1), 0, CAP)
    return ((ranking + rotation) % OBJ_DEV).astype(jnp.int32)


def touch_ends(entries, stream_key, low, top_value):
    place = [jax.random.randint(jax.random.fold_in(stream_key, axis), (), 0, length) for axis, length in enumerate(entries.shape)]
    main_axis = entries.shape.index(max(entries.shape))
    next_to = place[:main_axis] + [(place[main_axis] + 1) % entries.shape[main_axis]] + place[main_axis + 1:]
    return entries.at[tuple(place)].set(low).at[tuple(next_to)].set(top_value)


def levels(rng, dims, shards, least, top_value):
    def one(position, blocks):
        steps = jax.random.uniform(jax.random.fold_in(jax.random.fold_in(rng, 6), position), (blocks,), jnp.float32, least / len(shards), top_value / len(shards))
        return jnp.repeat(jnp.exp(steps), dims[position] // blocks).reshape((-1,) + (1,) * (len(dims) - position - 1))

    level = one(*shards[0])
    for cut in shards[1:]:
        level = level * one(*cut)
    return level


def gaussian(key, dims, deviation, most, cuts=(), kind=jnp.bfloat16):
    entries = deviation * jax.random.normal(key, dims, jnp.float32)
    if cuts:
        entries = entries * levels(key, dims, cuts, -0.22, 0.18)
    return jnp.clip(entries, -most, most).astype(kind)


def setup_inputs(seed: int = 0, part: int = 0) -> dict:
    key_list = jax.random.split(jax.random.key(seed), 12)
    part_splits = jax.random.split(jax.random.fold_in(key_list[11], part), 12)
    brightness = jnp.clip(jnp.exp(math.log(4.0) - 2.0794415 * jax.random.uniform(part_splits[0], (OBJ_TOTAL,), jnp.float32) ** levels(part_splits[0], (OBJ_TOTAL,), ((0, 16),), -0.2, 0.2)), 0.5, 4.0)
    subpixel = jnp.clip(1.0 * jax.random.uniform(part_splits[1], (2, OBJ_TOTAL), jnp.float32) ** levels(part_splits[1], (2, OBJ_TOTAL), ((1, 16),), -0.2, 0.2), 0.0, 1.0)
    profile_width = jnp.clip(jnp.exp(math.log(2.5) - 1.8325814 * jax.random.uniform(part_splits[2], (OBJ_TOTAL,), jnp.float32) ** levels(part_splits[2], (OBJ_TOTAL,), ((0, 16),), -0.2, 0.2)), 0.4, 2.5)
    psf_coef = gaussian(part_splits[3], (PSF_TERMS, OBJ_TOTAL), 1.0, 6.0, ((1, 16),))
    row_offset = touch_ends(jax.random.randint(part_splits[4], (OBJ_TOTAL,), 0 - STAMP // 2, H_DEV - STAMP // 2 + 1), jax.random.fold_in(part_splits[4], 1), 0 - STAMP // 2, (H_DEV - STAMP // 2 + 1) - 1).astype(jnp.int32)
    column_offset = touch_ends(jax.random.randint(part_splits[5], (OBJ_TOTAL,), 0, SENSOR_COLS - STAMP + 1), jax.random.fold_in(part_splits[5], 1), 0, SENSOR_COLS - STAMP).astype(jnp.int32)
    send_list = draw_send_list(jax.random.fold_in(jax.random.fold_in(key_list[11], part), 71), part)
    send_count = draw_send_count(jax.random.fold_in(jax.random.fold_in(key_list[11], part), 71), part)
    psf_basis = gaussian(key_list[8], (PSF_TERMS, STAMP, STAMP), PSF_TERMS ** -0.5, 1.25)
    vertical_kernel = jnp.clip(jax.random.uniform(key_list[9], (TAPS,), jnp.float32, 0.02, 0.2), 0.02, 0.2)
    horizontal_kernel = jnp.clip(jax.random.uniform(key_list[10], (TAPS,), jnp.float32, 0.02, 0.2), 0.02, 0.2)
    return {"brightness": brightness, "subpixel": subpixel, "profile_width": profile_width, "psf_coef": psf_coef, "row_offset": row_offset, "column_offset": column_offset, "send_list": send_list, "send_count": send_count, "psf_basis": psf_basis, "vertical_kernel": vertical_kernel, "horizontal_kernel": horizontal_kernel}


def profiles(offsets, widths, length):
    pixels = jnp.arange(length, dtype=jnp.float32)
    spacing = pixels[:, None] - pixels[None, :]
    distance = spacing[None, :, :] - offsets[:, None, None]
    spread = widths[:, None, None]
    values = jnp.exp(-distance * distance / (2.0 * spread * spread)) / (math.sqrt(2.0 * math.pi) * spread)
    return values.astype(jnp.bfloat16)

def render_stamps(coefficients, brightness, subpixel, profile_width, psf_basis):
    terms = psf_basis.shape[0]
    length = psf_basis.shape[1]
    flattened = psf_basis.reshape(terms, length * length)
    psf_images = jnp.dot(coefficients.T, flattened, preferred_element_type=jnp.float32)
    psf_images = lax.optimization_barrier(psf_images.astype(jnp.bfloat16)).reshape(-1, length, length)
    row_profile = lax.optimization_barrier(profiles(subpixel[0], profile_width, length))
    column_profile = lax.optimization_barrier(profiles(subpixel[1], profile_width, length))
    blurred = jnp.einsum('oij,ojk->oik', row_profile.astype(jnp.float32), psf_images.astype(jnp.float32))
    blurred = lax.optimization_barrier(blurred.astype(jnp.bfloat16))
    product = jnp.einsum('oik,olk->oil', blurred.astype(jnp.float32), column_profile.astype(jnp.float32))
    return (brightness[:, None, None] * product).astype(jnp.bfloat16)

def diffuse(plane, vertical_kernel, horizontal_kernel):
    tap_count = vertical_kernel.shape[0]
    radius = tap_count // 2
    height = plane.shape[0]
    breadth = plane.shape[1]
    padded = jnp.pad(plane, ((radius, radius), (0, 0)))
    smeared = vertical_kernel[0] * padded[0:height]
    for offset in range(1, tap_count):
        smeared = smeared + vertical_kernel[offset] * padded[offset:offset + height]
    wider = jnp.pad(smeared, ((0, 0), (radius, radius)))
    result = horizontal_kernel[0] * wider[:, 0:breadth]
    for offset in range(1, tap_count):
        result = result + horizontal_kernel[offset] * wider[:, offset:offset + breadth]
    return result

def reference(brightness, subpixel, profile_width, psf_coef, row_offset, column_offset, send_list, send_count, psf_basis, vertical_kernel, horizontal_kernel):
    cell_total = send_list.shape[0]
    capacity = send_list.shape[2]
    halfway = STAMP // 2
    canvas = jnp.zeros((ROWS_TOTAL + STAMP, SENSOR_COLS), jnp.float32)
    slot_ids = jnp.arange(capacity, dtype=jnp.int32)
    pixel_ids = jnp.arange(STAMP, dtype=jnp.int32)
    targets = jnp.repeat(jnp.arange(cell_total, dtype=jnp.int32), capacity)
    per_cell = (brightness.reshape(cell_total, OBJ_DEV), jnp.transpose(subpixel.reshape(2, cell_total, OBJ_DEV), (1, 0, 2)), profile_width.reshape(cell_total, OBJ_DEV), jnp.transpose(psf_coef.reshape(PSF_TERMS, cell_total, OBJ_DEV), (1, 0, 2)), row_offset.reshape(cell_total, OBJ_DEV), column_offset.reshape(cell_total, OBJ_DEV), send_list, send_count)

    def one_cell(board, pieces):
        cell_bright, cell_shift, cell_width, cell_coef, cell_rows, cell_columns, cell_list, cell_count = pieces
        stamps = render_stamps(cell_coef, cell_bright, cell_shift, cell_width, psf_basis)
        chosen = cell_list.reshape(-1).astype(jnp.int32)
        live = (slot_ids[None, :] < cell_count[:, None]).reshape(-1)
        picked = jnp.where(live[:, None, None], stamps[chosen], jnp.zeros((), jnp.bfloat16))
        top_rows = (targets * H_DEV + cell_rows[chosen] + halfway).astype(jnp.int32)
        left_columns = cell_columns[chosen].astype(jnp.int32)
        row_index = top_rows[:, None, None] + pixel_ids[None, :, None]
        column_index = left_columns[:, None, None] + pixel_ids[None, None, :]
        row_index = jnp.broadcast_to(row_index, picked.shape)
        column_index = jnp.broadcast_to(column_index, picked.shape)
        board = board.at[row_index, column_index].add(picked.astype(jnp.float32))
        return (board, None)
    canvas, _ = lax.scan(one_cell, canvas, per_cell)
    plane = canvas[halfway:halfway + ROWS_TOTAL]
    return diffuse(plane, vertical_kernel, horizontal_kernel)
```

```python
import functools
import math

import jax
import jax.numpy as jnp
from jax import lax
from jax.experimental import pallas as pl
from jax.experimental.pallas import tpu as pltpu
from jax.sharding import PartitionSpec as P

STAMP = 128
RADIUS = 4
LANES = 128
ROWS = STAMP + 2 * RADIUS
TABLE = 48
PIECES = 24
DEAD = -8.0
GROUP = 32
UNROLL = 4
BF = jnp.bfloat16
F32 = jnp.float32


def dot_nt(a, b):
    return lax.dot_general(a, b, (((1,), (1,)), ((), ())), preferred_element_type=F32)


def dot_nn(a, b):
    return jnp.dot(a, b, preferred_element_type=F32)


def pack_kernel(bright, sub, width, coef, row, col, slots, counts, out, work):
    cells, cap = slots.shape
    objects = bright.shape[1]
    terms = coef.shape[0]
    eye = lax.broadcasted_iota(jnp.int32, (cells, cells), 0) == lax.broadcasted_iota(
        jnp.int32, (cells, cells), 1
    )
    limit = jnp.sum(jnp.where(eye, counts[...].astype(F32), 0.0), axis=1, keepdims=True)
    lane = lax.broadcasted_iota(jnp.int32, (cells, LANES), 1)
    block = lax.broadcasted_iota(jnp.int32, (cells, LANES), 0).astype(F32) - DEAD
    hits = jnp.zeros((cells, LANES), F32)
    for c in range(cap):
        hit = (slots[:, c : c + 1] == lane) & (c < limit)
        hits = hits + jnp.where(hit, block, 0.0)
    target = jnp.sum(hits, axis=0, keepdims=True) + DEAD
    work[...] = jnp.zeros_like(work)
    work[0:terms, 0:objects] = coef[...].astype(F32)
    work[PIECES : PIECES + 1, 0:objects] = bright[...]
    work[PIECES + 1 : PIECES + 3, 0:objects] = sub[...]
    work[PIECES + 3 : PIECES + 4, 0:objects] = width[...]
    work[PIECES + 4 : PIECES + 5, 0:objects] = row[...].astype(F32)
    work[PIECES + 5 : PIECES + 6, 0:objects] = col[...].astype(F32)
    work[PIECES + 6 : PIECES + 7, :] = target
    full = work[PIECES : PIECES + 8, :]
    first = full.astype(BF).astype(F32)
    second = (full - first).astype(BF).astype(F32)
    work[PIECES : PIECES + 8, :] = first
    work[PIECES + 8 : PIECES + 16, :] = second
    work[PIECES + 16 : PIECES + 24, :] = full - first - second
    out[...] = work[...].astype(BF)


def band(weights, shape, flip):
    a = lax.broadcasted_iota(jnp.int32, shape, 0)
    b = lax.broadcasted_iota(jnp.int32, shape, 1)
    gap = a - b if flip else b - a
    total = jnp.zeros(shape, F32)
    for m in range(2 * RADIUS + 1):
        total = jnp.where(gap == m, weights[m], total)
    high = total.astype(BF)
    return high, (total - high.astype(F32)).astype(BF)


def render_kernel(
    position,
    vertical,
    horizontal,
    table,
    basis,
    out,
    canvas,
    images,
    stack,
    flat,
    wide,
    placed,
    onehot,
    coefs,
    reals,
    whole,
    reals_s,
    whole_s,
    smooth_hi,
    smooth_lo,
    sems,
):
    cells = table.shape[0] // TABLE
    terms = basis.shape[0]
    chunks = coefs.shape[0] // LANES
    me = position[0].astype(F32)
    last = position[1]

    stack[...] = jnp.zeros_like(stack)
    for k in range(0, terms, 2):
        even = basis[k].astype(F32)
        odd = basis[k + 1].astype(F32) if k + 1 < terms else jnp.zeros_like(even)
        for jb in range(STAMP // 8):
            both = jnp.concatenate(
                [even[8 * jb : 8 * jb + 8], odd[8 * jb : 8 * jb + 8]], axis=0
            )
            stack[8 * k : 8 * k + 16, LANES * jb : LANES * (jb + 1)] = both.astype(BF)

    wide[...] = jnp.zeros_like(wide)
    for d in range(cells):
        part = table[TABLE * d : TABLE * (d + 1), :]
        lanes = slice(LANES * d, LANES * (d + 1))
        flat[:, lanes] = part
        part = part.astype(F32)
        placed[d : d + 1, :] = part[PIECES + 6 : PIECES + 7, :]
        placed[cells + d : cells + d + 1, :] = part[PIECES + 4 : PIECES + 5, :]
        for k in range(0, terms, 2):
            pair = [jnp.broadcast_to(part[k : k + 1, :], (8, LANES))]
            pair.append(jnp.broadcast_to(part[k + 1 : k + 2, :], (8, LANES)))
            wide[8 * k : 8 * k + 16, lanes] = jnp.concatenate(pair, axis=0).astype(BF)

    top = (placed[0:cells, :] - me) * STAMP + placed[cells : 2 * cells, :] + RADIUS
    live = (top > -STAMP) & (top < ROWS)
    ones = jnp.where(live, 1.0, 0.0)
    upper = lax.broadcasted_iota(jnp.int32, (LANES, LANES), 0) <= lax.broadcasted_iota(
        jnp.int32, (LANES, LANES), 1
    )
    lower = lax.broadcasted_iota(jnp.int32, (cells, cells), 0) > lax.broadcasted_iota(
        jnp.int32, (cells, cells), 1
    )
    within_row = dot_nn(ones.astype(BF), jnp.where(upper, 1.0, 0.0).astype(BF))
    before = dot_nn(jnp.where(lower, 1.0, 0.0).astype(BF), ones.astype(BF))
    before = dot_nn(before.astype(BF), jnp.ones((LANES, LANES), BF))
    rank = jnp.where(live, within_row + before - 1.0, -1.0)
    placed[0:cells, :] = rank
    total = jnp.sum(ones).astype(jnp.int32)

    lane_f = lax.broadcasted_iota(jnp.int32, (1, LANES), 1).astype(F32)
    slot = lax.broadcasted_iota(jnp.int32, (LANES, LANES), 0).astype(F32)

    def compact(q, carry):
        start = (q * LANES).astype(F32)
        for d in range(cells):
            match = placed[d : d + 1, :] - start == slot
            onehot[:, LANES * d : LANES * (d + 1)] = jnp.where(match, 1.0, 0.0).astype(BF)
        hot = onehot[...]
        coefs[pl.ds(pl.multiple_of(q * LANES, LANES), LANES), :] = dot_nt(hot, wide[...])
        got = dot_nt(flat[...], hot)
        values = (
            got[PIECES : PIECES + 8] + got[PIECES + 8 : PIECES + 16] + got[PIECES + 16 : PIECES + 24]
        )
        valid = lane_f + start < total.astype(F32)
        spread = jnp.where(valid, values[3:4], 1.0)
        squared = spread * spread
        top_row = jnp.where(
            valid, (values[6:7] - me) * STAMP + values[4:5] + (RADIUS + STAMP), float(STAMP)
        )
        column = jnp.where(valid, values[5:6] + RADIUS, 0.0)
        top_8 = jnp.floor(top_row * 0.125) * 8.0
        tile = jnp.floor(column * (1.0 / LANES)) * LANES
        at = pl.ds(pl.multiple_of(q * 8, 8), 8)
        reals[at, :] = jnp.concatenate(
            [
                top_row - top_8 + values[1:2],
                values[2:3],
                (-0.5 / math.log(2.0)) / squared,
                jnp.where(valid, values[0:1], 0.0) / (2.0 * math.pi * squared),
                jnp.zeros((4, LANES), F32),
            ],
            axis=0,
        )
        whole[at, :] = jnp.concatenate(
            [top_8, top_row - top_8, tile, column - tile, jnp.zeros((4, LANES), F32)], axis=0
        ).astype(jnp.int32)
        return carry

    lax.fori_loop(0, (total + LANES - 1) // LANES, compact, 0)
    copy_r = pltpu.make_async_copy(reals, reals_s, sems.at[0])
    copy_w = pltpu.make_async_copy(whole, whole_s, sems.at[1])
    copy_r.start()
    copy_w.start()
    canvas[STAMP : STAMP + ROWS, :] = jnp.zeros((ROWS, canvas.shape[1]), F32)
    copy_r.wait()
    copy_w.wait()

    sub_i = lax.broadcasted_iota(jnp.int32, (8, LANES), 0)
    lane_i = lax.broadcasted_iota(jnp.int32, (8, LANES), 1)
    down = (sub_i - lane_i).astype(F32)
    diagonal = jnp.where((lane_i & 7) == sub_i, 1.0, 0.0)
    diagonal = jnp.concatenate([diagonal] * (coefs.shape[1] // LANES), axis=1)

    def group(g, carry):
        rows = coefs[pl.ds(pl.multiple_of(g * GROUP, GROUP), GROUP), :]
        spread = [
            jnp.broadcast_to(rows[i : i + 1, :], (8, rows.shape[1])) * diagonal
            for i in range(GROUP)
        ]
        images[...] = dot_nn(jnp.concatenate(spread, axis=0).astype(BF), stack[...])
        chunk8 = (g * GROUP) // LANES * 8
        first = g * GROUP - (g * GROUP) // LANES * LANES

        def several(u, inner):
            for v in range(UNROLL):
                i = u * UNROLL + v
                p = first + i
                shift_r = reals_s[chunk8, p]
                shift_c = reals_s[chunk8 + 1, p]
                sharp = reals_s[chunk8 + 2, p]
                scale = reals_s[chunk8 + 3, p]
                row_8 = pl.multiple_of(whole_s[chunk8, p], 8)
                edge = whole_s[chunk8 + 1, p]
                lane_0 = pl.multiple_of(whole_s[chunk8 + 2, p], LANES)
                turn = whole_s[chunk8 + 3, p]
                pixels = images[pl.ds(pl.multiple_of(i * 8, 8), 8), :]
                image = jnp.concatenate(
                    [pixels[:, LANES * jb : LANES * (jb + 1)] for jb in range(STAMP // 8)], axis=0
                ).astype(BF)
                gap = down - shift_r
                tiles = []
                for t in range(ROWS // 8):
                    far = gap + 8.0 * t
                    value = jnp.exp2(far * far * sharp)
                    if t == 0:
                        value = jnp.where(sub_i >= edge, value, 0.0)
                    if t == STAMP // 8:
                        value = jnp.where(sub_i < edge, value, 0.0)
                    tiles.append(value)
                by_rows = jnp.concatenate(tiles, axis=0).astype(BF)
                gap = -down - shift_c
                tiles = []
                for t in range(STAMP // 8):
                    far = gap - 8.0 * t
                    tiles.append(jnp.exp2(far * far * sharp))
                by_columns = jnp.concatenate(tiles, axis=0).astype(BF)
                blurred = dot_nn(by_rows, image).astype(BF)
                stamp = dot_nn(blurred, by_columns) * scale
                stamp = pltpu.roll(stamp, turn, 1)
                mine = lax.broadcasted_iota(jnp.int32, (ROWS, LANES), 1) >= turn
                here = pl.ds(row_8, ROWS)
                left = pl.ds(lane_0, LANES)
                right = pl.ds(lane_0 + LANES, LANES)
                canvas[here, left] = canvas[here, left] + jnp.where(mine, stamp, 0.0)
                canvas[here, right] = canvas[here, right] + jnp.where(mine, 0.0, stamp)
            return inner

        count = jnp.minimum(total - g * GROUP, GROUP)
        lax.fori_loop(0, (count + UNROLL - 1) // UNROLL, several, 0)
        return carry

    lax.fori_loop(0, (total + GROUP - 1) // GROUP, group, 0)

    @pl.when(position[0] == 0)
    def _():
        head = canvas[STAMP : STAMP + 8, :]
        keep = lax.broadcasted_iota(jnp.int32, head.shape, 0) >= RADIUS
        canvas[STAMP : STAMP + 8, :] = jnp.where(keep, head, 0.0)

    @pl.when(position[0] == last)
    def _():
        tail = canvas[STAMP + ROWS - 8 : STAMP + ROWS, :]
        keep = lax.broadcasted_iota(jnp.int32, tail.shape, 0) < RADIUS
        canvas[STAMP + ROWS - 8 : STAMP + ROWS, :] = jnp.where(keep, tail, 0.0)

    v_hi, v_lo = band(vertical, (STAMP, ROWS), False)
    h_hi, h_lo = band(horizontal, (2 * LANES, LANES), True)

    def smear(x, carry):
        at = pl.ds(pl.multiple_of(x * LANES, LANES), LANES)
        plane = canvas[STAMP : STAMP + ROWS, at]
        high = plane.astype(BF)
        low = (plane - high.astype(F32)).astype(BF)
        value = dot_nn(v_hi, high) + dot_nn(v_lo, high) + dot_nn(v_hi, low)
        high = value.astype(BF)
        smooth_hi[:, at] = high
        smooth_lo[:, at] = (value - high.astype(F32)).astype(BF)
        return carry

    lax.fori_loop(0, canvas.shape[1] // LANES, smear, 0)

    def across(x, carry):
        at = pl.ds(pl.multiple_of(x * LANES, LANES), 2 * LANES)
        high = smooth_hi[:, at]
        low = smooth_lo[:, at]
        out[:, pl.ds(pl.multiple_of(x * LANES, LANES), LANES)] = (
            dot_nn(high, h_hi) + dot_nn(high, h_lo) + dot_nn(low, h_hi)
        )
        return carry

    lax.fori_loop(0, out.shape[1] // LANES, across, 0)


def gather_all(table):
    count = lax.axis_size("row")
    if count & (count - 1):
        return lax.all_gather(table, "row", tiled=True)
    bit = 1
    while bit < count:
        other = lax.ppermute(table, "row", [(i, i ^ bit) for i in range(count)])
        table = jnp.concatenate([table, other], axis=0)
        bit *= 2
    return table


def on_device(
    brightness,
    subpixel,
    profile_width,
    psf_coef,
    row_offset,
    column_offset,
    send_list,
    send_count,
    psf_basis,
    vertical_kernel,
    horizontal_kernel,
    columns,
):
    cells = lax.axis_size("row")
    cap = send_list.shape[2]
    vmem = pl.BlockSpec(memory_space=pltpu.VMEM)
    smem = pl.BlockSpec(memory_space=pltpu.SMEM)
    table = pl.pallas_call(
        pack_kernel,
        out_shape=jax.ShapeDtypeStruct((TABLE, LANES), BF),
        in_specs=[vmem] * 8,
        out_specs=vmem,
        scratch_shapes=[pltpu.VMEM((TABLE, LANES), F32)],
        name="pack",
    )(
        brightness[None],
        subpixel,
        profile_width[None],
        psf_coef,
        row_offset[None],
        column_offset[None],
        send_list[0],
        send_count,
    )
    table = gather_all(table)
    position = jnp.stack([lax.axis_index("row"), jnp.int32(cells - 1)]).astype(jnp.int32)
    most = cells * min(3 * cap, brightness.shape[0])
    chunks = -(-most // LANES)
    breadth = columns + LANES
    kernel = pl.pallas_call(
        render_kernel,
        out_shape=jax.ShapeDtypeStruct((STAMP, columns), F32),
        in_specs=[smem, smem, smem, vmem, vmem],
        out_specs=vmem,
        scratch_shapes=[
            pltpu.VMEM((STAMP + 2 * ROWS, breadth), F32),
            pltpu.VMEM((8 * GROUP, STAMP * STAMP // 8), F32),
            pltpu.VMEM((256, STAMP * STAMP // 8), BF),
            pltpu.VMEM((TABLE, cells * LANES), BF),
            pltpu.VMEM((256, cells * LANES), BF),
            pltpu.VMEM((2 * cells, LANES), F32),
            pltpu.VMEM((LANES, cells * LANES), BF),
            pltpu.VMEM((chunks * LANES, 256), F32),
            pltpu.VMEM((chunks * 8, LANES), F32),
            pltpu.VMEM((chunks * 8, LANES), jnp.int32),
            pltpu.SMEM((chunks * 8, LANES), F32),
            pltpu.SMEM((chunks * 8, LANES), jnp.int32),
            pltpu.VMEM((STAMP, breadth), BF),
            pltpu.VMEM((STAMP, breadth), BF),
            pltpu.SemaphoreType.DMA((2,)),
        ],
        compiler_params=pltpu.CompilerParams(vmem_limit_bytes=48 * 1024 * 1024),
        name="render",
    )
    return kernel(position, vertical_kernel, horizontal_kernel, table, psf_basis)


def solution(mesh):
    in_specs = (
        P(("exp", "row")),
        P(None, ("exp", "row")),
        P(("exp", "row")),
        P(None, ("exp", "row")),
        P(("exp", "row")),
        P(("exp", "row")),
        P(("exp", "row"), None, None),
        P(("exp", "row"), None),
        P(),
        P(),
        P(),
    )
    return jax.shard_map(
        functools.partial(on_device, columns=4096),
        mesh=mesh,
        in_specs=in_specs,
        out_specs=P(("exp", "row"), None),
        check_vma=False,
    )
```

```python
import functools
import math

import jax
import jax.numpy as jnp
from jax import lax
from jax.experimental import pallas as pl
from jax.experimental.pallas import tpu as pltpu
from jax.sharding import PartitionSpec as P

STAMP = 128
RADIUS = 4
LANES = 128
ROWS = STAMP + 2 * RADIUS
TABLE = 48
PIECES = 24
DEAD = -8.0
GROUP = 32
UNROLL = 8
SPAN = 1024
BF = jnp.bfloat16
F32 = jnp.float32


def dot_nt(a, b):
    return lax.dot_general(a, b, (((1,), (1,)), ((), ())), preferred_element_type=F32)


def dot_nn(a, b):
    return jnp.dot(a, b, preferred_element_type=F32)


def pack_kernel(bright, sub, width, coef, row, col, slots, counts, out, work):
    cap, _, cells = slots.shape
    objects = bright.shape[1]
    terms = coef.shape[0]
    eye = lax.broadcasted_iota(jnp.int32, (cells, cells), 0) == lax.broadcasted_iota(
        jnp.int32, (cells, cells), 1
    )
    limit = jnp.sum(jnp.where(eye, counts[...].astype(F32), 0.0), axis=1, keepdims=True)
    lane = lax.broadcasted_iota(jnp.int32, (cells, LANES), 1).astype(F32)
    block = lax.broadcasted_iota(jnp.int32, (cells, LANES), 0).astype(F32) - DEAD
    hits = jnp.zeros((cells, LANES), F32)
    for c in range(cap):
        entry = jnp.sum(jnp.where(eye, slots[c].astype(F32), 0.0), axis=1, keepdims=True)
        hit = (entry == lane) & (c < limit)
        hits = hits + jnp.where(hit, block, 0.0)
    target = jnp.sum(hits, axis=0, keepdims=True) + DEAD
    work[...] = jnp.zeros_like(work)
    work[0:terms, 0:objects] = coef[...].astype(F32)
    work[PIECES : PIECES + 1, 0:objects] = bright[...]
    work[PIECES + 1 : PIECES + 3, 0:objects] = sub[...]
    work[PIECES + 3 : PIECES + 4, 0:objects] = width[...]
    work[PIECES + 4 : PIECES + 5, 0:objects] = row[...].astype(F32)
    work[PIECES + 5 : PIECES + 6, 0:objects] = col[...].astype(F32)
    work[PIECES + 6 : PIECES + 7, :] = target
    full = work[PIECES : PIECES + 8, :]
    first = full.astype(BF).astype(F32)
    second = (full - first).astype(BF).astype(F32)
    work[PIECES : PIECES + 8, :] = first
    work[PIECES + 8 : PIECES + 16, :] = second
    work[PIECES + 16 : PIECES + 24, :] = full - first - second
    out[...] = work[...].astype(BF)


def band(weights, shape, flip):
    a = lax.broadcasted_iota(jnp.int32, shape, 0)
    b = lax.broadcasted_iota(jnp.int32, shape, 1)
    gap = a - b if flip else b - a
    total = jnp.zeros(shape, F32)
    for m in range(2 * RADIUS + 1):
        total = jnp.where(gap == m, weights[m], total)
    return total.astype(BF)


def prepare_kernel(vertical, horizontal, basis, stack, down_band, side_band):
    terms = basis.shape[0]
    down_band[...] = band(vertical, down_band.shape, False)
    side_band[...] = band(horizontal, side_band.shape, True)
    for k in range(0, stack.shape[0] // 8, 2):
        if k >= terms:
            stack[8 * k : 8 * k + 16, :] = jnp.zeros((16, stack.shape[1]), BF)
            continue
        even = basis[k].astype(F32)
        odd = basis[k + 1].astype(F32) if k + 1 < terms else jnp.zeros_like(even)
        for jb in range(STAMP // 8):
            both = jnp.concatenate(
                [even[8 * jb : 8 * jb + 8], odd[8 * jb : 8 * jb + 8]], axis=0
            )
            stack[8 * k : 8 * k + 16, LANES * jb : LANES * (jb + 1)] = both.astype(BF)


def render_kernel(
    table,
    stack,
    down_band,
    side_band,
    out,
    canvas,
    images,
    flat,
    wide,
    placed,
    onehot,
    by_rows,
    blurred,
    by_columns,
    coefs,
    reals,
    whole,
    reals_s,
    whole_s,
    smooth,
    result,
    sems,
):
    cells = table.shape[0] // TABLE
    position = lax.axis_index("row")
    me = position.astype(F32)
    canvas[STAMP : STAMP + ROWS, :] = jnp.zeros((ROWS, canvas.shape[1]), F32)

    wide[...] = jnp.zeros_like(wide)
    for d in range(cells):
        part = table[TABLE * d : TABLE * (d + 1), :]
        lanes = slice(LANES * d, LANES * (d + 1))
        flat[:, lanes] = part
        part = part.astype(F32)
        placed[d : d + 1, :] = part[PIECES + 6 : PIECES + 7, :]
        placed[cells + d : cells + d + 1, :] = part[PIECES + 4 : PIECES + 5, :]
        for k in range(0, PIECES, 2):
            pair = [jnp.broadcast_to(part[k : k + 1, :], (8, LANES))]
            pair.append(jnp.broadcast_to(part[k + 1 : k + 2, :], (8, LANES)))
            wide[8 * k : 8 * k + 16, lanes] = jnp.concatenate(pair, axis=0).astype(BF)

    top = (placed[0:cells, :] - me) * STAMP + placed[cells : 2 * cells, :] + RADIUS
    live = (top > -STAMP) & (top < ROWS)
    ones = jnp.where(live, 1.0, 0.0)
    upper = lax.broadcasted_iota(jnp.int32, (LANES, LANES), 0) <= lax.broadcasted_iota(
        jnp.int32, (LANES, LANES), 1
    )
    lower = lax.broadcasted_iota(jnp.int32, (cells, cells), 0) > lax.broadcasted_iota(
        jnp.int32, (cells, cells), 1
    )
    within_row = dot_nn(ones.astype(BF), jnp.where(upper, 1.0, 0.0).astype(BF))
    before = dot_nn(jnp.where(lower, 1.0, 0.0).astype(BF), ones.astype(BF))
    before = dot_nn(before.astype(BF), jnp.ones((LANES, LANES), BF))
    rank = jnp.where(live, within_row + before - 1.0, -1.0)
    placed[0:cells, :] = rank
    total = jnp.sum(ones).astype(jnp.int32)

    lane_f = lax.broadcasted_iota(jnp.int32, (1, LANES), 1).astype(F32)
    slot = lax.broadcasted_iota(jnp.int32, (LANES, LANES), 0).astype(F32)

    def compact(q, carry):
        start = (q * LANES).astype(F32)
        for d in range(cells):
            match = placed[d : d + 1, :] - start == slot
            onehot[:, LANES * d : LANES * (d + 1)] = jnp.where(match, 1.0, 0.0).astype(BF)
        hot = onehot[...]
        coefs[pl.ds(pl.multiple_of(q * LANES, LANES), LANES), :] = dot_nt(hot, wide[...])
        got = dot_nt(flat[...], hot)
        values = (
            got[PIECES : PIECES + 8] + got[PIECES + 8 : PIECES + 16] + got[PIECES + 16 : PIECES + 24]
        )
        valid = lane_f + start < total.astype(F32)
        spread = jnp.where(valid, values[3:4], 1.0)
        squared = spread * spread
        top_row = jnp.where(
            valid, (values[6:7] - me) * STAMP + values[4:5] + (RADIUS + STAMP), float(STAMP)
        )
        column = jnp.where(valid, values[5:6] + RADIUS, 0.0)
        top_8 = jnp.floor(top_row * 0.125) * 8.0
        tile = jnp.floor(column * (1.0 / LANES)) * LANES
        at = pl.ds(pl.multiple_of(q * 8, 8), 8)
        reals[at, :] = jnp.concatenate(
            [
                top_row - top_8 + values[1:2],
                values[2:3],
                (-0.5 / math.log(2.0)) / squared,
                jnp.where(valid, values[0:1], 0.0) / (2.0 * math.pi * squared),
                jnp.zeros((4, LANES), F32),
            ],
            axis=0,
        )
        whole[at, :] = jnp.concatenate(
            [top_8, top_row - top_8, tile, column - tile, jnp.zeros((4, LANES), F32)], axis=0
        ).astype(jnp.int32)
        return carry

    lax.fori_loop(0, (total + LANES - 1) // LANES, compact, 0)
    copy_r = pltpu.make_async_copy(reals, reals_s, sems.at[0])
    copy_w = pltpu.make_async_copy(whole, whole_s, sems.at[1])
    copy_r.start()
    copy_w.start()
    copy_r.wait()
    copy_w.wait()

    sub_i = lax.broadcasted_iota(jnp.int32, (8, LANES), 0)
    lane_i = lax.broadcasted_iota(jnp.int32, (8, LANES), 1)
    down = (sub_i - lane_i).astype(F32)
    diagonal = jnp.where((lane_i & 7) == sub_i, 1.0, 0.0)
    diagonal = jnp.concatenate([diagonal] * (coefs.shape[1] // LANES), axis=1)

    def group(g, carry):
        rows = coefs[pl.ds(pl.multiple_of(g * GROUP, GROUP), GROUP), :]
        spread = [
            jnp.broadcast_to(rows[i : i + 1, :], (8, rows.shape[1])) * diagonal
            for i in range(GROUP)
        ]
        pixels = dot_nn(jnp.concatenate(spread, axis=0).astype(BF), stack[...])
        for i in range(GROUP):
            image = [
                pixels[8 * i : 8 * i + 8, LANES * jb : LANES * (jb + 1)] for jb in range(STAMP // 8)
            ]
            images[g * GROUP + i] = jnp.concatenate(image, axis=0).astype(BF)
        return carry

    lax.fori_loop(0, (total + GROUP - 1) // GROUP, group, 0)

    def params(s):
        p = jnp.maximum(s, 0) * UNROLL
        return (p >> 7) << 3, p & (LANES - 1), p

    def toeplitz(base, shift, sharp, factor):
        halves = []
        for start in (-float(LANES), 0.0):
            pieces = []
            for row in (0.0, 8.0):
                far = base + (start - row)
                far = far - shift
                value = jnp.exp2(far * far * sharp)
                pieces.append(value if factor is None else value * factor)
            halves.append(jnp.concatenate(pieces, axis=0).astype(BF))
        return halves

    def make_rows(s):
        r, c, _ = params(s)
        for v in range(UNROLL):
            shift = reals_s[r, c + v]
            sharp = reals_s[r + 2, c + v]
            edge = whole_s[r + 1, c + v]
            before, after = toeplitz(across_16, -shift, sharp, None)
            lanes = slice(LANES * (v % 2), LANES * (v % 2 + 1))
            by_rows[v // 2, 0:16, lanes] = jnp.where(sub_16 >= edge, after, zero_16)
            for t in range(1, STAMP // 16):
                both = jnp.where(lane_16 < LANES - 16 * t, after, before)
                by_rows[v // 2, 16 * t : 16 * t + 16, lanes] = pltpu.roll(both, 16 * t, 1)
            by_rows[v // 2, STAMP : STAMP + 16, lanes] = jnp.where(sub_16 < edge, before, zero_16)

    def make_columns(s):
        r, c, _ = params(s)
        for v in range(UNROLL):
            shift = reals_s[r + 1, c + v]
            sharp = reals_s[r + 2, c + v]
            scale = reals_s[r + 3, c + v]
            turn = whole_s[r + 3, c + v]
            before, after = toeplitz(across_16, shift, sharp, scale)
            mine = lane_16 >= turn
            for t in range(STAMP // 16):
                both = after if t == 0 else jnp.where(lane_16 < LANES - 16 * t, after, before)
                both = pltpu.roll(both, (turn + 16 * t) & (LANES - 1), 1)
                by_columns[v, 16 * t : 16 * t + 16, 0:LANES] = jnp.where(mine, both, zero_16)
                by_columns[v, 16 * t : 16 * t + 16, LANES:] = jnp.where(mine, zero_16, both)

    across_16 = (lane_i - sub_i).astype(F32)
    lane_16 = lax.broadcasted_iota(jnp.int32, (16, LANES), 1)
    sub_16 = lax.broadcasted_iota(jnp.int32, (16, LANES), 0)
    zero_16 = jnp.zeros((16, LANES), BF)
    nothing = jnp.zeros((LANES, LANES), BF)

    def blocks(a, b):
        return jnp.concatenate(
            [jnp.concatenate([a, nothing], axis=1), jnp.concatenate([nothing, b], axis=1)], axis=0
        )

    def blur(s):
        _, _, p = params(s)
        for w in range(0, UNROLL, 2):
            pair = blocks(images[p + w], images[p + w + 1])
            blurred[w // 2] = dot_nn(by_rows[w // 2], pair).astype(BF)

    def place(s):
        r, c, _ = params(s)
        for v in range(UNROLL):
            row_8 = pl.multiple_of(whole_s[r, c + v], 8)
            lane_0 = pl.multiple_of(whole_s[r + 2, c + v], LANES)
            stamp = dot_nn(blurred[v // 2, :, LANES * (v % 2) : LANES * (v % 2 + 1)], by_columns[v])
            window = canvas.at[pl.ds(row_8, ROWS), pl.ds(lane_0, 2 * LANES)]
            window[...] = window[...] + stamp[0:ROWS]

    blurred[...] = jnp.zeros_like(blurred)
    by_columns[...] = jnp.zeros_like(by_columns)
    by_rows[...] = jnp.zeros_like(by_rows)
    turns = (total + UNROLL - 1) // UNROLL

    def step(s, carry):
        place(s - 2)
        blur(s - 1)
        make_columns(s - 1)
        make_rows(s)
        return carry

    lax.fori_loop(0, jnp.where(total > 0, turns + 2, 0), step, 0)

    @pl.when(position == 0)
    def _():
        head = canvas[STAMP : STAMP + 8, :]
        keep = lax.broadcasted_iota(jnp.int32, head.shape, 0) >= RADIUS
        canvas[STAMP : STAMP + 8, :] = jnp.where(keep, head, 0.0)

    @pl.when(position == cells - 1)
    def _():
        tail = canvas[STAMP + ROWS - 8 : STAMP + ROWS, :]
        keep = lax.broadcasted_iota(jnp.int32, tail.shape, 0) < RADIUS
        canvas[STAMP + ROWS - 8 : STAMP + ROWS, :] = jnp.where(keep, tail, 0.0)

    columns = result.shape[1]
    spans = columns // SPAN
    copies = []
    for x in range(spans + 1):
        if x < spans:
            stop = columns + LANES if x == spans - 1 else (x + 1) * SPAN
            plane = canvas[STAMP : STAMP + ROWS, x * SPAN : stop].astype(BF)
            smooth[:, x * SPAN : stop] = dot_nn(down_band[...], plane).astype(BF)
        if x > 0:
            for y in range((x - 1) * SPAN, x * SPAN, LANES):
                result[:, y : y + LANES] = dot_nn(smooth[:, y : y + 2 * LANES], side_band[...])
            ready = slice((x - 1) * SPAN, x * SPAN)
            copy = pltpu.make_async_copy(
                result.at[:, ready], out.at[:, ready], sems.at[1 + x]
            )
            copy.start()
            copies.append(copy)
    for copy in copies:
        copy.wait()


def gather_all(table):
    count = lax.axis_size("row")
    if count & (count - 1):
        return lax.all_gather(table, "row", tiled=True)
    bit = 1
    while bit < count:
        other = lax.ppermute(table, "row", [(i, i ^ bit) for i in range(count)])
        table = jnp.concatenate([table, other], axis=0)
        bit *= 2
    return table


def on_device(
    brightness,
    subpixel,
    profile_width,
    psf_coef,
    row_offset,
    column_offset,
    send_list,
    send_count,
    psf_basis,
    vertical_kernel,
    horizontal_kernel,
    columns,
):
    cells = lax.axis_size("row")
    cap = send_list.shape[2]
    vmem = pl.BlockSpec(memory_space=pltpu.VMEM)
    smem = pl.BlockSpec(memory_space=pltpu.SMEM)
    table = pl.pallas_call(
        pack_kernel,
        out_shape=pltpu.VMEM((TABLE, LANES), BF),
        in_specs=[vmem] * 8,
        out_specs=vmem,
        scratch_shapes=[pltpu.VMEM((TABLE, LANES), F32)],
        name="pack",
    )(
        brightness[None],
        subpixel,
        profile_width[None],
        psf_coef,
        row_offset[None],
        column_offset[None],
        jnp.transpose(send_list, (2, 0, 1)),
        send_count,
    )
    prepared = pl.pallas_call(
        prepare_kernel,
        out_shape=(
            pltpu.VMEM((8 * 32, STAMP * STAMP // 8), BF),
            pltpu.VMEM((STAMP, ROWS), BF),
            pltpu.VMEM((2 * LANES, LANES), BF),
        ),
        in_specs=[smem, smem, vmem],
        out_specs=(vmem, vmem, vmem),
        cost_estimate=pl.CostEstimate(flops=0, bytes_accessed=2000000, transcendentals=0),
        name="prepare",
    )(vertical_kernel, horizontal_kernel, psf_basis)
    table = gather_all(table)
    most = cells * min(3 * cap, brightness.shape[0])
    chunks = -(-most // LANES)
    breadth = columns + LANES
    kernel = pl.pallas_call(
        render_kernel,
        out_shape=jax.ShapeDtypeStruct((STAMP, columns), F32),
        in_specs=[vmem] * 4,
        out_specs=pl.BlockSpec(memory_space=pl.ANY),
        scratch_shapes=[
            pltpu.VMEM((STAMP + 2 * ROWS, breadth), F32),
            pltpu.VMEM(((chunks + 1) * LANES, STAMP, STAMP), BF),
            pltpu.VMEM((TABLE, cells * LANES), BF),
            pltpu.VMEM((8 * 32, cells * LANES), BF),
            pltpu.VMEM((2 * cells, LANES), F32),
            pltpu.VMEM((LANES, cells * LANES), BF),
            pltpu.VMEM((UNROLL // 2, ROWS + 8, 2 * LANES), BF),
            pltpu.VMEM((UNROLL // 2, ROWS + 8, 2 * LANES), BF),
            pltpu.VMEM((UNROLL, LANES, 2 * LANES), BF),
            pltpu.VMEM((chunks * LANES, 8 * 32), F32),
            pltpu.VMEM((chunks * 8 + 8, LANES), F32),
            pltpu.VMEM((chunks * 8 + 8, LANES), jnp.int32),
            pltpu.SMEM((chunks * 8 + 8, LANES), F32),
            pltpu.SMEM((chunks * 8 + 8, LANES), jnp.int32),
            pltpu.VMEM((STAMP, breadth), BF),
            pltpu.VMEM((STAMP, columns), F32),
            pltpu.SemaphoreType.DMA((2 + columns // SPAN,)),
        ],
        compiler_params=pltpu.CompilerParams(vmem_limit_bytes=44 * 1024 * 1024),
        name="render",
    )
    return kernel(table, *prepared)


def solution(mesh):
    in_specs = (
        P(("exp", "row")),
        P(None, ("exp", "row")),
        P(("exp", "row")),
        P(None, ("exp", "row")),
        P(("exp", "row")),
        P(("exp", "row")),
        P(("exp", "row"), None, None),
        P(("exp", "row"), None),
        P(),
        P(),
        P(),
    )
    return jax.shard_map(
        functools.partial(on_device, columns=4096),
        mesh=mesh,
        in_specs=in_specs,
        out_specs=P(("exp", "row"), None),
        check_vma=False,
    )
```

```python
import functools
import math

import jax
import jax.numpy as jnp
from jax import lax
from jax.experimental import pallas as pl
from jax.experimental.pallas import tpu as pltpu
from jax.sharding import PartitionSpec as P

STAMP = 128
RADIUS = 4
LANES = 128
ROWS = STAMP + 2 * RADIUS
TABLE = 48
PIECES = 24
DEAD = -8.0
GROUP = 64
UNROLL = 8
SPAN = 1024
BF = jnp.bfloat16
F32 = jnp.float32


def dot_nt(a, b):
    return lax.dot_general(a, b, (((1,), (1,)), ((), ())), preferred_element_type=F32)


def dot_nn(a, b):
    return jnp.dot(a, b, preferred_element_type=F32)


def pack_kernel(bright, sub, width, coef, row, col, slots, counts, out, work):
    cap, _, cells = slots.shape
    objects = bright.shape[1]
    terms = coef.shape[0]
    eye = lax.broadcasted_iota(jnp.int32, (cells, cells), 0) == lax.broadcasted_iota(
        jnp.int32, (cells, cells), 1
    )
    limit = jnp.sum(jnp.where(eye, counts[...].astype(F32), 0.0), axis=1, keepdims=True)
    lane = lax.broadcasted_iota(jnp.int32, (cells, LANES), 1).astype(F32)
    block = lax.broadcasted_iota(jnp.int32, (cells, LANES), 0).astype(F32) - DEAD
    hits = jnp.zeros((cells, LANES), F32)
    for c in range(cap):
        entry = jnp.sum(jnp.where(eye, slots[c].astype(F32), 0.0), axis=1, keepdims=True)
        hit = (entry == lane) & (c < limit)
        hits = hits + jnp.where(hit, block, 0.0)
    target = jnp.sum(hits, axis=0, keepdims=True) + DEAD
    work[...] = jnp.zeros_like(work)
    work[0:terms, 0:objects] = coef[...].astype(F32)
    work[PIECES : PIECES + 1, 0:objects] = bright[...]
    work[PIECES + 1 : PIECES + 3, 0:objects] = sub[...]
    work[PIECES + 3 : PIECES + 4, 0:objects] = width[...]
    work[PIECES + 4 : PIECES + 5, 0:objects] = row[...].astype(F32)
    work[PIECES + 5 : PIECES + 6, 0:objects] = col[...].astype(F32)
    work[PIECES + 6 : PIECES + 7, :] = target
    full = work[PIECES : PIECES + 8, :]
    first = full.astype(BF).astype(F32)
    second = (full - first).astype(BF).astype(F32)
    work[PIECES : PIECES + 8, :] = first
    work[PIECES + 8 : PIECES + 16, :] = second
    work[PIECES + 16 : PIECES + 24, :] = full - first - second
    out[...] = work[...].astype(BF)


def band(weights, shape, flip):
    a = lax.broadcasted_iota(jnp.int32, shape, 0)
    b = lax.broadcasted_iota(jnp.int32, shape, 1)
    gap = a - b if flip else b - a
    total = jnp.zeros(shape, F32)
    for m in range(2 * RADIUS + 1):
        total = jnp.where(gap == m, weights[m], total)
    return total.astype(BF)


def prepare_kernel(vertical, horizontal, basis, stack, down_band, side_band):
    terms = basis.shape[0]
    down_band[...] = band(vertical, down_band.shape, False)
    side_band[...] = band(horizontal, side_band.shape, True)
    for k in range(0, stack.shape[0] // 8, 2):
        if k >= terms:
            stack[8 * k : 8 * k + 16, :] = jnp.zeros((16, stack.shape[1]), BF)
            continue
        even = basis[k].astype(F32)
        odd = basis[k + 1].astype(F32) if k + 1 < terms else jnp.zeros_like(even)
        for jb in range(STAMP // 8):
            both = jnp.concatenate(
                [even[8 * jb : 8 * jb + 8], odd[8 * jb : 8 * jb + 8]], axis=0
            )
            stack[8 * k : 8 * k + 16, LANES * jb : LANES * (jb + 1)] = both.astype(BF)


def render_kernel(
    table,
    stack,
    down_band,
    side_band,
    out,
    canvas,
    images,
    flat,
    wide,
    placed,
    sorted_in,
    onehot,
    by_rows,
    blurred,
    by_columns,
    coefs,
    reals,
    whole,
    reals_s,
    whole_s,
    smooth,
    result,
    sems,
):
    cells = table.shape[0] // TABLE
    position = lax.axis_index("row")
    me = position.astype(F32)
    canvas[...] = jnp.zeros_like(canvas)
    tiles = canvas.shape[1] // LANES - 1

    wide[...] = jnp.zeros_like(wide)
    tile_ids = lax.broadcasted_iota(jnp.int32, (tiles, LANES), 0).astype(F32)
    for d in range(cells):
        part = table[TABLE * d : TABLE * (d + 1), :]
        lanes = slice(LANES * d, LANES * (d + 1))
        flat[:, lanes] = part
        part = part.astype(F32)
        whole_part = (
            part[PIECES : PIECES + 8] + part[PIECES + 8 : PIECES + 16] + part[PIECES + 16 : TABLE]
        )
        top = (whole_part[6:7] - me) * STAMP + whole_part[4:5] + RADIUS
        live = (top > -STAMP) & (top < ROWS)
        tile = jnp.floor((whole_part[5:6] + RADIUS) * (1.0 / LANES))
        tile = jnp.where(live, tile, -1.0)
        same = tile_ids == jnp.broadcast_to(tile, (tiles, LANES))
        sorted_in[tiles * d : tiles * (d + 1), :] = jnp.where(same, 1.0, 0.0).astype(BF)
        for k in range(0, PIECES, 2):
            pair = [jnp.broadcast_to(part[k : k + 1, :], (8, LANES))]
            pair.append(jnp.broadcast_to(part[k + 1 : k + 2, :], (8, LANES)))
            wide[8 * k : 8 * k + 16, lanes] = jnp.concatenate(pair, axis=0).astype(BF)

    upper = lax.broadcasted_iota(jnp.int32, (LANES, LANES), 0) <= lax.broadcasted_iota(
        jnp.int32, (LANES, LANES), 1
    )
    lower = lax.broadcasted_iota(jnp.int32, (tiles, tiles), 0) > lax.broadcasted_iota(
        jnp.int32, (tiles, tiles), 1
    )
    sums = jnp.concatenate(
        [jnp.where(upper, 1.0, 0.0).astype(BF), jnp.ones((LANES, LANES), BF)], axis=1
    )
    ranks = dot_nn(sorted_in[...], sums)
    before = jnp.zeros((tiles, LANES), F32)
    orders = []
    for d in range(cells):
        mine = slice(tiles * d, tiles * (d + 1))
        orders.append(ranks[mine, 0:LANES] + before)
        before = before + ranks[mine, LANES:]
    pairs = jnp.floor((before + 1.0) * 0.5)
    base = 2.0 * dot_nn(jnp.where(lower, 1.0, 0.0).astype(BF), pairs.astype(BF))
    for d in range(cells):
        mine = sorted_in[tiles * d : tiles * (d + 1), :].astype(F32)
        placed[d : d + 1, :] = jnp.sum(mine * (orders[d] + base), axis=0, keepdims=True) - 1.0
    total = (jnp.sum(pairs) * (2.0 / LANES)).astype(jnp.int32)

    slot = lax.broadcasted_iota(jnp.int32, (LANES, LANES), 0).astype(F32)

    def compact(q, carry):
        start = (q * LANES).astype(F32)
        for d in range(cells):
            match = placed[d : d + 1, :] - start == slot
            onehot[:, LANES * d : LANES * (d + 1)] = jnp.where(match, 1.0, 0.0).astype(BF)
        hot = onehot[...]
        coefs[pl.ds(pl.multiple_of(q * LANES, LANES), LANES), :] = dot_nt(hot, wide[...])
        got = dot_nt(flat[...], hot)
        values = (
            got[PIECES : PIECES + 8] + got[PIECES + 8 : PIECES + 16] + got[PIECES + 16 : PIECES + 24]
        )
        valid = values[3:4] > 0.0
        spread = jnp.where(valid, values[3:4], 1.0)
        squared = spread * spread
        top_row = jnp.where(valid, (values[6:7] - me) * STAMP + values[4:5] + RADIUS, 0.0)
        column = jnp.where(valid, values[5:6] + RADIUS, 0.0)
        top_16 = jnp.floor(top_row * 0.0625) * 16.0
        tile = jnp.floor(column * (1.0 / LANES)) * LANES
        at = pl.ds(pl.multiple_of(q * 8, 8), 8)
        reals[at, :] = jnp.concatenate(
            [
                top_row - top_16 + values[1:2],
                values[2:3],
                (-0.5 / math.log(2.0)) / squared,
                jnp.where(valid, values[0:1], 0.0) / (2.0 * math.pi * squared),
                jnp.zeros((4, LANES), F32),
            ],
            axis=0,
        )
        whole[at, :] = jnp.concatenate(
            [
                top_16 + STAMP,
                top_row - top_16,
                tile,
                column - tile,
                jnp.zeros((4, LANES), F32),
            ],
            axis=0,
        ).astype(jnp.int32)
        return carry

    lax.fori_loop(0, (total + LANES - 1) // LANES, compact, 0)
    copy_r = pltpu.make_async_copy(reals, reals_s, sems.at[0])
    copy_w = pltpu.make_async_copy(whole, whole_s, sems.at[1])
    copy_r.start()
    copy_w.start()
    copy_r.wait()
    copy_w.wait()

    sub_i = lax.broadcasted_iota(jnp.int32, (8, LANES), 0)
    lane_i = lax.broadcasted_iota(jnp.int32, (8, LANES), 1)
    down = (sub_i - lane_i).astype(F32)
    diagonal = jnp.where((lane_i & 7) == sub_i, 1.0, 0.0)
    diagonal = jnp.concatenate([diagonal] * (coefs.shape[1] // LANES), axis=1)

    def group(g, carry):
        rows = coefs[pl.ds(pl.multiple_of(g * GROUP, GROUP), GROUP), :]
        spread = [
            jnp.broadcast_to(rows[i : i + 1, :], (8, rows.shape[1])) * diagonal
            for i in range(GROUP)
        ]
        pixels = dot_nn(jnp.concatenate(spread, axis=0).astype(BF), stack[...])
        for i in range(GROUP):
            image = [
                pixels[8 * i : 8 * i + 8, LANES * jb : LANES * (jb + 1)] for jb in range(STAMP // 8)
            ]
            images[g * GROUP + i] = jnp.concatenate(image, axis=0).astype(BF)
        return carry

    lax.fori_loop(0, (total + GROUP - 1) // GROUP, group, 0)

    def params(s):
        p = jnp.maximum(s, 0) * UNROLL
        return (p >> 7) << 3, p & (LANES - 1), p

    def toeplitz(base, shift, sharp, factor):
        halves = []
        for start in (-float(LANES), 0.0):
            pieces = []
            for row in (0.0, 8.0):
                far = base + (start - row)
                far = far - shift
                value = jnp.exp2(far * far * sharp)
                pieces.append(value if factor is None else value * factor)
            halves.append(jnp.concatenate(pieces, axis=0).astype(BF))
        return halves

    def make_rows(s, pair):
        r, c, _ = params(s)
        for v in (pair, pair + 1):
            shift = reals_s[r, c + v]
            sharp = reals_s[r + 2, c + v]
            edge = whole_s[r + 1, c + v]
            before, after = toeplitz(across_16, -shift, sharp, None)
            lanes = slice(LANES * (v % 2), LANES * (v % 2 + 1))
            row_16 = pl.multiple_of(whole_s[r, c + v], 16)
            for t in range((ROWS + 8) // 16):
                by_rows[v // 2, STAMP + 16 * t : STAMP + 16 * t + 16, lanes] = zero_16
            strip = by_rows.at[v // 2, pl.ds(row_16, ROWS + 8), lanes]
            for t in range(STAMP // 16 + 1):
                if t == 0:
                    rows_16 = jnp.where(sub_16 >= edge, after, zero_16)
                elif t == STAMP // 16:
                    rows_16 = jnp.where(sub_16 < edge, before, zero_16)
                else:
                    both = jnp.where(lane_16 < LANES - 16 * t, after, before)
                    rows_16 = pltpu.roll(both, 16 * t, 1)
                strip[16 * t : 16 * t + 16, :] = rows_16

    def make_columns(s, pair):
        r, c, _ = params(s)
        for v in (pair, pair + 1):
            shift = reals_s[r + 1, c + v]
            sharp = reals_s[r + 2, c + v]
            scale = reals_s[r + 3, c + v]
            turn = whole_s[r + 3, c + v]
            before, after = toeplitz(across_16, shift, sharp, scale)
            mine = lane_16 >= turn
            first = LANES * (v % 2)
            for t in range(STAMP // 16):
                both = after if t == 0 else jnp.where(lane_16 < LANES - 16 * t, after, before)
                both = pltpu.roll(both, (turn + 16 * t) & (LANES - 1), 1)
                by_columns[v // 2, first + 16 * t : first + 16 * t + 16, 0:LANES] = jnp.where(mine, both, zero_16)
                by_columns[v // 2, first + 16 * t : first + 16 * t + 16, LANES:] = jnp.where(mine, zero_16, both)

    across_16 = (lane_i - sub_i).astype(F32)
    lane_16 = lax.broadcasted_iota(jnp.int32, (16, LANES), 1)
    sub_16 = lax.broadcasted_iota(jnp.int32, (16, LANES), 0)
    zero_16 = jnp.zeros((16, LANES), BF)
    nothing = jnp.zeros((LANES, LANES), BF)

    def blocks(a, b):
        return jnp.concatenate(
            [jnp.concatenate([a, nothing], axis=1), jnp.concatenate([nothing, b], axis=1)], axis=0
        )

    def blur(s, w):
        _, _, p = params(s)
        pair = blocks(images[p + w], images[p + w + 1])
        blurred[w // 2] = dot_nn(
            by_rows[w // 2, STAMP : STAMP + ROWS + 8, :], pair
        ).astype(BF)

    def place(s, w):
        r, c, _ = params(s)
        lane_0 = pl.multiple_of(whole_s[r + 2, c + w], LANES)
        stamp = dot_nn(blurred[w // 2], by_columns[w // 2])
        window = canvas.at[:, pl.ds(lane_0, 2 * LANES)]
        window[...] = window[...] + stamp[0:ROWS]

    blurred[...] = jnp.zeros_like(blurred)
    by_columns[...] = jnp.zeros_like(by_columns)
    by_rows[...] = jnp.zeros_like(by_rows)
    turns = (total + UNROLL - 1) // UNROLL

    def step(s, carry):
        for w in range(0, UNROLL, 2):
            place(s - 2, w)
            blur(s - 1, w)
            make_columns(s - 1, w)
            make_rows(s, w)
        return carry

    lax.fori_loop(0, jnp.where(total > 0, turns + 2, 0), step, 0)

    @pl.when(position == 0)
    def _():
        head = canvas[0:8, :]
        keep = lax.broadcasted_iota(jnp.int32, head.shape, 0) >= RADIUS
        canvas[0:8, :] = jnp.where(keep, head, 0.0)

    @pl.when(position == cells - 1)
    def _():
        tail = canvas[ROWS - 8 : ROWS, :]
        keep = lax.broadcasted_iota(jnp.int32, tail.shape, 0) < RADIUS
        canvas[ROWS - 8 : ROWS, :] = jnp.where(keep, tail, 0.0)

    columns = result.shape[1]
    spans = columns // SPAN
    copies = []
    for x in range(spans + 1):
        if x < spans:
            stop = columns + LANES if x == spans - 1 else (x + 1) * SPAN
            plane = canvas[:, x * SPAN : stop].astype(BF)
            smooth[:, x * SPAN : stop] = dot_nn(down_band[...], plane).astype(BF)
        if x > 0:
            starts = range((x - 1) * SPAN, x * SPAN, LANES)
            tall = jnp.concatenate([smooth[:, y : y + 2 * LANES] for y in starts], axis=0)
            tall = dot_nn(tall, side_band[...])
            for i, y in enumerate(starts):
                result[:, y : y + LANES] = tall[STAMP * i : STAMP * (i + 1)]
            ready = slice((x - 1) * SPAN, x * SPAN)
            copy = pltpu.make_async_copy(
                result.at[:, ready], out.at[:, ready], sems.at[1 + x]
            )
            copy.start()
            copies.append(copy)
    for copy in copies:
        copy.wait()


def gather_all(table, prepared):
    count = lax.axis_size("row")
    if count & (count - 1):
        return lax.all_gather(table, "row", tiled=True), prepared
    rounds = [(2, 4, 6)] if count > 4 else [(bit,) for bit in (2,) if bit < count]
    rounds += [(1 << b,) for b in range(3, count.bit_length() - 1)] + [(1,)] * (count > 1)
    for masks in rounds:
        others = [
            lax.ppermute(table, "row", [(i, i ^ mask) for i in range(count)]) for mask in masks
        ]
        table = jnp.concatenate([table] + others, axis=0)
        if masks is rounds[0]:
            table, prepared = lax.optimization_barrier((table, prepared))
    return table, prepared


def on_device(
    brightness,
    subpixel,
    profile_width,
    psf_coef,
    row_offset,
    column_offset,
    send_list,
    send_count,
    psf_basis,
    vertical_kernel,
    horizontal_kernel,
    columns,
):
    cells = lax.axis_size("row")
    cap = send_list.shape[2]
    vmem = pl.BlockSpec(memory_space=pltpu.VMEM)
    smem = pl.BlockSpec(memory_space=pltpu.SMEM)
    table = pl.pallas_call(
        pack_kernel,
        out_shape=pltpu.VMEM((TABLE, LANES), BF),
        in_specs=[vmem] * 8,
        out_specs=vmem,
        scratch_shapes=[pltpu.VMEM((TABLE, LANES), F32)],
        name="pack",
    )(
        brightness[None],
        subpixel,
        profile_width[None],
        psf_coef,
        row_offset[None],
        column_offset[None],
        jnp.transpose(send_list, (2, 0, 1)),
        send_count,
    )
    prepared = pl.pallas_call(
        prepare_kernel,
        out_shape=(
            pltpu.VMEM((8 * 32, STAMP * STAMP // 8), BF),
            pltpu.VMEM((STAMP, ROWS), BF),
            pltpu.VMEM((2 * LANES, LANES), BF),
        ),
        in_specs=[smem, smem, vmem],
        out_specs=(vmem, vmem, vmem),
        cost_estimate=pl.CostEstimate(flops=0, bytes_accessed=2000000, transcendentals=0),
        name="prepare",
    )(vertical_kernel, horizontal_kernel, psf_basis)
    table, prepared = gather_all(table, prepared)
    most = cells * min(3 * cap, brightness.shape[0]) + columns // LANES
    chunks = -(-most // LANES)
    breadth = columns + LANES
    kernel = pl.pallas_call(
        render_kernel,
        out_shape=jax.ShapeDtypeStruct((STAMP, columns), F32),
        in_specs=[vmem] * 4,
        out_specs=pl.BlockSpec(memory_space=pl.ANY),
        scratch_shapes=[
            pltpu.VMEM((ROWS, breadth), F32),
            pltpu.VMEM(((chunks + 1) * LANES, STAMP, STAMP), BF),
            pltpu.VMEM((TABLE, cells * LANES), BF),
            pltpu.VMEM((8 * 32, cells * LANES), BF),
            pltpu.VMEM((cells, LANES), F32),
            pltpu.VMEM((cells * columns // LANES, LANES), BF),
            pltpu.VMEM((LANES, cells * LANES), BF),
            pltpu.VMEM((UNROLL // 2, 2 * STAMP + ROWS + 8, 2 * LANES), BF),
            pltpu.VMEM((UNROLL // 2, ROWS + 8, 2 * LANES), BF),
            pltpu.VMEM((UNROLL // 2, 2 * LANES, 2 * LANES), BF),
            pltpu.VMEM((chunks * LANES, 8 * 32), F32),
            pltpu.VMEM((chunks * 8 + 8, LANES), F32),
            pltpu.VMEM((chunks * 8 + 8, LANES), jnp.int32),
            pltpu.SMEM((chunks * 8 + 8, LANES), F32),
            pltpu.SMEM((chunks * 8 + 8, LANES), jnp.int32),
            pltpu.VMEM((STAMP, breadth), BF),
            pltpu.VMEM((STAMP, columns), F32),
            pltpu.SemaphoreType.DMA((2 + columns // SPAN,)),
        ],
        compiler_params=pltpu.CompilerParams(vmem_limit_bytes=44 * 1024 * 1024),
        name="render",
    )
    return kernel(table, *prepared)


def solution(mesh):
    in_specs = (
        P(("exp", "row")),
        P(None, ("exp", "row")),
        P(("exp", "row")),
        P(None, ("exp", "row")),
        P(("exp", "row")),
        P(("exp", "row")),
        P(("exp", "row"), None, None),
        P(("exp", "row"), None),
        P(),
        P(),
        P(),
    )
    return jax.shard_map(
        functools.partial(on_device, columns=4096),
        mesh=mesh,
        in_specs=in_specs,
        out_specs=P(("exp", "row"), None),
        check_vma=False,
    )
```

```python
import functools
import math

import jax
import jax.numpy as jnp
from jax import lax
from jax.experimental import pallas as pl
from jax.experimental.pallas import tpu as pltpu
from jax.sharding import PartitionSpec as P

STAMP = 128
RADIUS = 4
LANES = 128
ROWS = STAMP + 2 * RADIUS
TABLE = 48
PIECES = 24
DEAD = -8.0
GROUP = 64
UNROLL = 8
SPAN = 1024
BF = jnp.bfloat16
F32 = jnp.float32


def dot_nt(a, b):
    return lax.dot_general(a, b, (((1,), (1,)), ((), ())), preferred_element_type=F32)


def dot_nn(a, b):
    return jnp.dot(a, b, preferred_element_type=F32)


def pack_kernel(bright, sub, width, coef, row, col, slots, counts, out, work):
    cap, _, cells = slots.shape
    objects = bright.shape[1]
    terms = coef.shape[0]
    eye = lax.broadcasted_iota(jnp.int32, (cells, cells), 0) == lax.broadcasted_iota(
        jnp.int32, (cells, cells), 1
    )
    limit = jnp.sum(jnp.where(eye, counts[...].astype(F32), 0.0), axis=1, keepdims=True)
    lane = lax.broadcasted_iota(jnp.int32, (cells, LANES), 1).astype(F32)
    block = lax.broadcasted_iota(jnp.int32, (cells, LANES), 0).astype(F32) - DEAD
    hits = jnp.zeros((cells, LANES), F32)
    for c in range(cap):
        entry = jnp.sum(jnp.where(eye, slots[c].astype(F32), 0.0), axis=1, keepdims=True)
        hit = (entry == lane) & (c < limit)
        hits = hits + jnp.where(hit, block, 0.0)
    target = jnp.sum(hits, axis=0, keepdims=True) + DEAD
    work[...] = jnp.zeros_like(work)
    work[0:terms, 0:objects] = coef[...].astype(F32)
    work[PIECES : PIECES + 1, 0:objects] = bright[...]
    work[PIECES + 1 : PIECES + 3, 0:objects] = sub[...]
    work[PIECES + 3 : PIECES + 4, 0:objects] = width[...]
    work[PIECES + 4 : PIECES + 5, 0:objects] = row[...].astype(F32)
    work[PIECES + 5 : PIECES + 6, 0:objects] = col[...].astype(F32)
    work[PIECES + 6 : PIECES + 7, :] = target
    full = work[PIECES : PIECES + 8, :]
    first = full.astype(BF).astype(F32)
    second = (full - first).astype(BF).astype(F32)
    work[PIECES : PIECES + 8, :] = first
    work[PIECES + 8 : PIECES + 16, :] = second
    work[PIECES + 16 : PIECES + 24, :] = full - first - second
    out[...] = work[...].astype(BF)


def band(weights, shape, flip):
    a = lax.broadcasted_iota(jnp.int32, shape, 0)
    b = lax.broadcasted_iota(jnp.int32, shape, 1)
    gap = a - b if flip else b - a
    total = jnp.zeros(shape, F32)
    for m in range(2 * RADIUS + 1):
        total = jnp.where(gap == m, weights[m], total)
    return total.astype(BF)


def prepare_kernel(vertical, horizontal, basis, stack, down_band, side_band):
    terms = basis.shape[0]
    down_band[...] = band(vertical, down_band.shape, False)
    side_band[...] = band(horizontal, side_band.shape, True)
    for k in range(0, stack.shape[0] // 8, 2):
        if k >= terms:
            stack[8 * k : 8 * k + 16, :] = jnp.zeros((16, stack.shape[1]), BF)
            continue
        even = basis[k].astype(F32)
        odd = basis[k + 1].astype(F32) if k + 1 < terms else jnp.zeros_like(even)
        for jb in range(STAMP // 8):
            both = jnp.concatenate(
                [even[8 * jb : 8 * jb + 8], odd[8 * jb : 8 * jb + 8]], axis=0
            )
            stack[8 * k : 8 * k + 16, LANES * jb : LANES * (jb + 1)] = both.astype(BF)


def render_kernel(
    table,
    stack,
    down_band,
    side_band,
    out,
    canvas,
    images,
    flat,
    placed,
    sorted_in,
    onehot,
    by_rows,
    blurred,
    by_columns,
    coefs,
    reals,
    whole,
    reals_s,
    whole_s,
    smooth,
    result,
    sems,
):
    cells = table.shape[0] // TABLE
    position = lax.axis_index("row")
    me = position.astype(F32)
    canvas[...] = jnp.zeros_like(canvas)
    tiles = canvas.shape[1] // LANES - 1

    tile_ids = lax.broadcasted_iota(jnp.int32, (tiles, LANES), 0).astype(F32)
    for d in range(cells):
        part = table[TABLE * d : TABLE * (d + 1), :]
        lanes = slice(LANES * d, LANES * (d + 1))
        flat[:, lanes] = part
        part = part.astype(F32)
        whole_part = (
            part[PIECES : PIECES + 8] + part[PIECES + 8 : PIECES + 16] + part[PIECES + 16 : TABLE]
        )
        top = (whole_part[6:7] - me) * STAMP + whole_part[4:5] + RADIUS
        live = (top > -STAMP) & (top < ROWS)
        tile = jnp.floor((whole_part[5:6] + RADIUS) * (1.0 / LANES))
        tile = jnp.where(live, tile, -1.0)
        same = tile_ids == jnp.broadcast_to(tile, (tiles, LANES))
        sorted_in[tiles * d : tiles * (d + 1), :] = jnp.where(same, 1.0, 0.0).astype(BF)

    upper = lax.broadcasted_iota(jnp.int32, (LANES, LANES), 0) <= lax.broadcasted_iota(
        jnp.int32, (LANES, LANES), 1
    )
    lower = lax.broadcasted_iota(jnp.int32, (tiles, tiles), 0) > lax.broadcasted_iota(
        jnp.int32, (tiles, tiles), 1
    )
    sums = jnp.concatenate(
        [jnp.where(upper, 1.0, 0.0).astype(BF), jnp.ones((LANES, LANES), BF)], axis=1
    )
    ranks = dot_nn(sorted_in[...], sums)
    before = jnp.zeros((tiles, LANES), F32)
    orders = []
    for d in range(cells):
        mine = slice(tiles * d, tiles * (d + 1))
        orders.append(ranks[mine, 0:LANES] + before)
        before = before + ranks[mine, LANES:]
    pairs = jnp.floor((before + 1.0) * 0.5)
    base = 2.0 * dot_nn(jnp.where(lower, 1.0, 0.0).astype(BF), pairs.astype(BF))
    for d in range(cells):
        mine = sorted_in[tiles * d : tiles * (d + 1), :].astype(F32)
        placed[d : d + 1, :] = jnp.sum(mine * (orders[d] + base), axis=0, keepdims=True) - 1.0
    total = (jnp.sum(pairs) * (2.0 / LANES)).astype(jnp.int32)

    slot = lax.broadcasted_iota(jnp.int32, (LANES, LANES), 0).astype(F32)
    eighth = lax.broadcasted_iota(jnp.int32, (32, coefs.shape[1]), 1) >> 3
    repeat = eighth == lax.broadcasted_iota(jnp.int32, eighth.shape, 0)
    repeat = jnp.where(repeat & (eighth < PIECES), 1.0, 0.0).astype(BF)

    def compact(q, carry):
        start = (q * LANES).astype(F32)
        for d in range(cells):
            match = placed[d : d + 1, :] - start == slot
            onehot[:, LANES * d : LANES * (d + 1)] = jnp.where(match, 1.0, 0.0).astype(BF)
        hot = onehot[...]
        got = dot_nt(flat[...], hot)
        coefs[pl.ds(pl.multiple_of(q * LANES, LANES), LANES), :] = lax.dot_general(
            got[0:32].astype(BF), repeat, (((0,), (0,)), ((), ())), preferred_element_type=F32
        )
        values = (
            got[PIECES : PIECES + 8] + got[PIECES + 8 : PIECES + 16] + got[PIECES + 16 : PIECES + 24]
        )
        valid = values[3:4] > 0.0
        spread = jnp.where(valid, values[3:4], 1.0)
        squared = spread * spread
        top_row = jnp.where(valid, (values[6:7] - me) * STAMP + values[4:5] + RADIUS, 0.0)
        column = jnp.where(valid, values[5:6] + RADIUS, 0.0)
        top_16 = jnp.floor(top_row * 0.0625) * 16.0
        tile = jnp.floor(column * (1.0 / LANES)) * LANES
        at = pl.ds(pl.multiple_of(q * 8, 8), 8)
        reals[at, :] = jnp.concatenate(
            [
                top_row - top_16 + values[1:2],
                values[2:3],
                (-0.5 / math.log(2.0)) / squared,
                jnp.where(valid, values[0:1], 0.0) / (2.0 * math.pi * squared),
                jnp.zeros((4, LANES), F32),
            ],
            axis=0,
        )
        whole[at, :] = jnp.concatenate(
            [
                top_16 + STAMP,
                top_row - top_16,
                tile,
                column - tile,
                jnp.zeros((4, LANES), F32),
            ],
            axis=0,
        ).astype(jnp.int32)
        return carry

    lax.fori_loop(0, (total + LANES - 1) // LANES, compact, 0)
    copy_r = pltpu.make_async_copy(reals, reals_s, sems.at[0])
    copy_w = pltpu.make_async_copy(whole, whole_s, sems.at[1])
    copy_r.start()
    copy_w.start()

    sub_i = lax.broadcasted_iota(jnp.int32, (8, LANES), 0)
    lane_i = lax.broadcasted_iota(jnp.int32, (8, LANES), 1)
    down = (sub_i - lane_i).astype(F32)
    diagonal = jnp.where((lane_i & 7) == sub_i, 1.0, 0.0)
    diagonal = jnp.concatenate([diagonal] * (coefs.shape[1] // LANES), axis=1)

    def group(g, carry):
        rows = coefs[pl.ds(pl.multiple_of(g * GROUP, GROUP), GROUP), :]
        spread = [
            jnp.broadcast_to(rows[i : i + 1, :], (8, rows.shape[1])) * diagonal
            for i in range(GROUP)
        ]
        pixels = dot_nn(jnp.concatenate(spread, axis=0).astype(BF), stack[...])
        for i in range(GROUP):
            image = [
                pixels[8 * i : 8 * i + 8, LANES * jb : LANES * (jb + 1)] for jb in range(STAMP // 8)
            ]
            images[g * GROUP + i] = jnp.concatenate(image, axis=0).astype(BF)
        return carry

    lax.fori_loop(0, (total + GROUP - 1) // GROUP, group, 0)

    copy_r.wait()
    copy_w.wait()

    def params(s):
        p = s * UNROLL
        return (p >> 7) << 3, p & (LANES - 1), p

    def toeplitz(base, shift, sharp, factor):
        halves = []
        for start in (-float(LANES), 0.0):
            pieces = []
            for row in (0.0, 8.0):
                far = base + (start - row)
                far = far - shift
                value = jnp.exp2(far * far * sharp)
                pieces.append(value if factor is None else value * factor)
            halves.append(jnp.concatenate(pieces, axis=0).astype(BF))
        return halves

    def make_rows(s, pair):
        r, c, _ = params(s)
        for v in (pair, pair + 1):
            shift = reals_s[r, c + v]
            sharp = reals_s[r + 2, c + v]
            edge = whole_s[r + 1, c + v]
            before, after = toeplitz(across_16, -shift, sharp, None)
            lanes = slice(LANES * (v % 2), LANES * (v % 2 + 1))
            row_16 = pl.multiple_of(whole_s[r, c + v], 16)
            for t in range((ROWS + 8) // 16):
                by_rows[v // 2, STAMP + 16 * t : STAMP + 16 * t + 16, lanes] = zero_16
            strip = by_rows.at[v // 2, pl.ds(row_16, ROWS + 8), lanes]
            for t in range(STAMP // 16 + 1):
                if t == 0:
                    rows_16 = jnp.where(sub_16 >= edge, after, zero_16)
                elif t == STAMP // 16:
                    rows_16 = jnp.where(sub_16 < edge, before, zero_16)
                else:
                    both = jnp.where(lane_16 < LANES - 16 * t, after, before)
                    rows_16 = pltpu.roll(both, 16 * t, 1)
                strip[16 * t : 16 * t + 16, :] = rows_16

    def make_columns(s, pair):
        r, c, _ = params(s)
        for v in (pair, pair + 1):
            shift = reals_s[r + 1, c + v]
            sharp = reals_s[r + 2, c + v]
            scale = reals_s[r + 3, c + v]
            turn = whole_s[r + 3, c + v]
            before, after = toeplitz(across_16, shift, sharp, scale)
            mine = lane_16 >= turn
            first = LANES * (v % 2)
            for t in range(STAMP // 16):
                both = after if t == 0 else jnp.where(lane_16 < LANES - 16 * t, after, before)
                both = pltpu.roll(both, (turn + 16 * t) & (LANES - 1), 1)
                by_columns[v // 2, first + 16 * t : first + 16 * t + 16, 0:LANES] = jnp.where(mine, both, zero_16)
                by_columns[v // 2, first + 16 * t : first + 16 * t + 16, LANES:] = jnp.where(mine, zero_16, both)

    across_16 = (lane_i - sub_i).astype(F32)
    lane_16 = lax.broadcasted_iota(jnp.int32, (16, LANES), 1)
    sub_16 = lax.broadcasted_iota(jnp.int32, (16, LANES), 0)
    zero_16 = jnp.zeros((16, LANES), BF)
    nothing = jnp.zeros((LANES, LANES), BF)

    def blocks(a, b):
        return jnp.concatenate(
            [jnp.concatenate([a, nothing], axis=1), jnp.concatenate([nothing, b], axis=1)], axis=0
        )

    def blur(s, w):
        _, _, p = params(s)
        pair = blocks(images[p + w], images[p + w + 1])
        blurred[w // 2] = dot_nn(
            by_rows[w // 2, STAMP : STAMP + ROWS + 8, :], pair
        ).astype(BF)

    def place(s, w):
        r, c, _ = params(s)
        lane_0 = pl.multiple_of(whole_s[r + 2, c + w], LANES)
        stamp = dot_nn(blurred[w // 2], by_columns[w // 2])
        window = canvas.at[:, pl.ds(lane_0, 2 * LANES)]
        window[...] = window[...] + stamp[0:ROWS]

    turns = jnp.maximum((total + UNROLL - 1) // UNROLL, 2)

    @pl.when(total > 0)
    def _():
        for w in range(0, UNROLL, 2):
            make_rows(0, w)
        for w in range(0, UNROLL, 2):
            blur(0, w)
            make_columns(0, w)
            make_rows(1, w)

        def step(s, carry):
            for w in range(0, UNROLL, 2):
                place(s - 2, w)
                blur(s - 1, w)
                make_columns(s - 1, w)
                make_rows(s, w)
            return carry

        lax.fori_loop(2, turns, step, 0)
        for w in range(0, UNROLL, 2):
            place(turns - 2, w)
            blur(turns - 1, w)
            make_columns(turns - 1, w)
        for w in range(0, UNROLL, 2):
            place(turns - 1, w)

    @pl.when(position == 0)
    def _():
        head = canvas[0:8, :]
        keep = lax.broadcasted_iota(jnp.int32, head.shape, 0) >= RADIUS
        canvas[0:8, :] = jnp.where(keep, head, 0.0)

    @pl.when(position == cells - 1)
    def _():
        tail = canvas[ROWS - 8 : ROWS, :]
        keep = lax.broadcasted_iota(jnp.int32, tail.shape, 0) < RADIUS
        canvas[ROWS - 8 : ROWS, :] = jnp.where(keep, tail, 0.0)

    columns = result.shape[1]
    spans = columns // SPAN
    copies = []
    for x in range(spans + 1):
        if x < spans:
            stop = columns + LANES if x == spans - 1 else (x + 1) * SPAN
            plane = canvas[:, x * SPAN : stop].astype(BF)
            smooth[:, x * SPAN : stop] = dot_nn(down_band[...], plane).astype(BF)
        if x > 0:
            starts = range((x - 1) * SPAN, x * SPAN, LANES)
            tall = jnp.concatenate([smooth[:, y : y + 2 * LANES] for y in starts], axis=0)
            tall = dot_nn(tall, side_band[...])
            for i, y in enumerate(starts):
                result[:, y : y + LANES] = tall[STAMP * i : STAMP * (i + 1)]
            ready = slice((x - 1) * SPAN, x * SPAN)
            copy = pltpu.make_async_copy(
                result.at[:, ready], out.at[:, ready], sems.at[1 + x]
            )
            copy.start()
            copies.append(copy)
    for copy in copies:
        copy.wait()


def gather_all(table, prepared):
    count = lax.axis_size("row")
    if count & (count - 1):
        return lax.all_gather(table, "row", tiled=True), prepared
    rounds = [(2, 4, 6)] if count > 4 else [(bit,) for bit in (2,) if bit < count]
    rounds += [(1 << b,) for b in range(3, count.bit_length() - 1)] + [(1,)] * (count > 1)
    for masks in rounds:
        others = [
            lax.ppermute(table, "row", [(i, i ^ mask) for i in range(count)]) for mask in masks
        ]
        table = jnp.concatenate([table] + others, axis=0)
        if masks is rounds[0]:
            table, prepared = lax.optimization_barrier((table, prepared))
    return table, prepared


def on_device(
    brightness,
    subpixel,
    profile_width,
    psf_coef,
    row_offset,
    column_offset,
    send_list,
    send_count,
    psf_basis,
    vertical_kernel,
    horizontal_kernel,
    columns,
):
    cells = lax.axis_size("row")
    cap = send_list.shape[2]
    vmem = pl.BlockSpec(memory_space=pltpu.VMEM)
    smem = pl.BlockSpec(memory_space=pltpu.SMEM)
    table = pl.pallas_call(
        pack_kernel,
        out_shape=pltpu.VMEM((TABLE, LANES), BF),
        in_specs=[vmem] * 8,
        out_specs=vmem,
        scratch_shapes=[pltpu.VMEM((TABLE, LANES), F32)],
        name="pack",
    )(
        brightness[None],
        subpixel,
        profile_width[None],
        psf_coef,
        row_offset[None],
        column_offset[None],
        jnp.transpose(send_list, (2, 0, 1)),
        send_count,
    )
    prepared = pl.pallas_call(
        prepare_kernel,
        out_shape=(
            pltpu.VMEM((8 * 32, STAMP * STAMP // 8), BF),
            pltpu.VMEM((STAMP, ROWS), BF),
            pltpu.VMEM((2 * LANES, LANES), BF),
        ),
        in_specs=[smem, smem, vmem],
        out_specs=(vmem, vmem, vmem),
        cost_estimate=pl.CostEstimate(flops=0, bytes_accessed=2000000, transcendentals=0),
        name="prepare",
    )(vertical_kernel, horizontal_kernel, psf_basis)
    table, prepared = gather_all(table, prepared)
    most = cells * min(3 * cap, brightness.shape[0]) + columns // LANES
    chunks = -(-most // LANES)
    breadth = columns + LANES
    kernel = pl.pallas_call(
        render_kernel,
        out_shape=jax.ShapeDtypeStruct((STAMP, columns), F32),
        in_specs=[vmem] * 4,
        out_specs=pl.BlockSpec(memory_space=pl.ANY),
        scratch_shapes=[
            pltpu.VMEM((ROWS, breadth), F32),
            pltpu.VMEM(((chunks + 1) * LANES, STAMP, STAMP), BF),
            pltpu.VMEM((TABLE, cells * LANES), BF),
            pltpu.VMEM((cells, LANES), F32),
            pltpu.VMEM((cells * columns // LANES, LANES), BF),
            pltpu.VMEM((LANES, cells * LANES), BF),
            pltpu.VMEM((UNROLL // 2, 2 * STAMP + ROWS + 8, 2 * LANES), BF),
            pltpu.VMEM((UNROLL // 2, ROWS + 8, 2 * LANES), BF),
            pltpu.VMEM((UNROLL // 2, 2 * LANES, 2 * LANES), BF),
            pltpu.VMEM((chunks * LANES, 8 * 32), F32),
            pltpu.VMEM((chunks * 8 + 8, LANES), F32),
            pltpu.VMEM((chunks * 8 + 8, LANES), jnp.int32),
            pltpu.SMEM((chunks * 8 + 8, LANES), F32),
            pltpu.SMEM((chunks * 8 + 8, LANES), jnp.int32),
            pltpu.VMEM((STAMP, breadth), BF),
            pltpu.VMEM((STAMP, columns), F32),
            pltpu.SemaphoreType.DMA((2 + columns // SPAN,)),
        ],
        compiler_params=pltpu.CompilerParams(vmem_limit_bytes=44 * 1024 * 1024),
        name="render",
    )
    return kernel(table, *prepared)


def solution(mesh):
    in_specs = (
        P(("exp", "row")),
        P(None, ("exp", "row")),
        P(("exp", "row")),
        P(None, ("exp", "row")),
        P(("exp", "row")),
        P(("exp", "row")),
        P(("exp", "row"), None, None),
        P(("exp", "row"), None),
        P(),
        P(),
        P(),
    )
    return jax.shard_map(
        functools.partial(on_device, columns=4096),
        mesh=mesh,
        in_specs=in_specs,
        out_specs=P(("exp", "row"), None),
        check_vma=False,
    )
```

```python
import functools
import math

import jax
import jax.numpy as jnp
from jax import lax
from jax.experimental import pallas as pl
from jax.experimental.pallas import tpu as pltpu
from jax.sharding import PartitionSpec as P

STAMP = 128
RADIUS = 4
LANES = 128
ROWS = STAMP + 2 * RADIUS
TABLE = 48
PIECES = 24
DEAD = -8.0
GROUP = 64
UNROLL = 8
SPAN = 1024
BF = jnp.bfloat16
F32 = jnp.float32


def dot_nt(a, b):
    return lax.dot_general(a, b, (((1,), (1,)), ((), ())), preferred_element_type=F32)


def dot_nn(a, b):
    return jnp.dot(a, b, preferred_element_type=F32)


def pack_kernel(bright, sub, width, coef, row, col, slots, counts, out, work):
    cap, _, cells = slots.shape
    objects = bright.shape[1]
    terms = coef.shape[0]
    eye = lax.broadcasted_iota(jnp.int32, (cells, cells), 0) == lax.broadcasted_iota(
        jnp.int32, (cells, cells), 1
    )
    limit = jnp.sum(jnp.where(eye, counts[...].astype(F32), 0.0), axis=1, keepdims=True)
    lane = lax.broadcasted_iota(jnp.int32, (cells, LANES), 1).astype(F32)
    block = lax.broadcasted_iota(jnp.int32, (cells, LANES), 0).astype(F32) - DEAD
    hits = jnp.zeros((cells, LANES), F32)
    for c in range(cap):
        entry = jnp.sum(jnp.where(eye, slots[c].astype(F32), 0.0), axis=1, keepdims=True)
        hit = (entry == lane) & (c < limit)
        hits = hits + jnp.where(hit, block, 0.0)
    target = jnp.sum(hits, axis=0, keepdims=True) + DEAD
    work[...] = jnp.zeros_like(work)
    work[0:terms, 0:objects] = coef[...].astype(F32)
    work[PIECES : PIECES + 1, 0:objects] = bright[...]
    work[PIECES + 1 : PIECES + 3, 0:objects] = sub[...]
    work[PIECES + 3 : PIECES + 4, 0:objects] = width[...]
    work[PIECES + 4 : PIECES + 5, 0:objects] = row[...].astype(F32)
    work[PIECES + 5 : PIECES + 6, 0:objects] = col[...].astype(F32)
    work[PIECES + 6 : PIECES + 7, :] = target
    full = work[PIECES : PIECES + 8, :]
    first = full.astype(BF).astype(F32)
    second = (full - first).astype(BF).astype(F32)
    work[PIECES : PIECES + 8, :] = first
    work[PIECES + 8 : PIECES + 16, :] = second
    work[PIECES + 16 : PIECES + 24, :] = full - first - second
    out[...] = work[...].astype(BF)


def band(weights, shape, flip):
    a = lax.broadcasted_iota(jnp.int32, shape, 0)
    b = lax.broadcasted_iota(jnp.int32, shape, 1)
    gap = a - b if flip else b - a
    total = jnp.zeros(shape, F32)
    for m in range(2 * RADIUS + 1):
        total = jnp.where(gap == m, weights[m], total)
    return total.astype(BF)


def prepare_kernel(vertical, horizontal, basis, stack, down_band, side_band, plane):
    terms = basis.shape[0]
    plane[...] = jnp.zeros_like(plane)
    down_band[...] = band(vertical, down_band.shape, False)
    side_band[...] = band(horizontal, side_band.shape, True)
    for k in range(0, stack.shape[0] // 8, 2):
        if k >= terms:
            stack[8 * k : 8 * k + 16, :] = jnp.zeros((16, stack.shape[1]), BF)
            continue
        even = basis[k].astype(F32)
        odd = basis[k + 1].astype(F32) if k + 1 < terms else jnp.zeros_like(even)
        for jb in range(STAMP // 8):
            both = jnp.concatenate(
                [even[8 * jb : 8 * jb + 8], odd[8 * jb : 8 * jb + 8]], axis=0
            )
            stack[8 * k : 8 * k + 16, LANES * jb : LANES * (jb + 1)] = both.astype(BF)


def render_kernel(
    table,
    stack,
    down_band,
    side_band,
    plane,
    out,
    canvas,
    images,
    flat,
    placed,
    sorted_in,
    onehot,
    by_rows,
    blurred,
    by_columns,
    coefs,
    reals,
    whole,
    reals_s,
    whole_s,
    smooth,
    result,
    sems,
):
    cells = table.shape[0] // TABLE
    position = lax.axis_index("row")
    me = position.astype(F32)
    tiles = canvas.shape[1] // LANES - 1

    tile_ids = lax.broadcasted_iota(jnp.int32, (tiles, LANES), 0).astype(F32)
    for d in range(cells):
        part = table[TABLE * d : TABLE * (d + 1), :]
        lanes = slice(LANES * d, LANES * (d + 1))
        flat[:, lanes] = part
        part = part.astype(F32)
        whole_part = (
            part[PIECES : PIECES + 8] + part[PIECES + 8 : PIECES + 16] + part[PIECES + 16 : TABLE]
        )
        top = (whole_part[6:7] - me) * STAMP + whole_part[4:5] + RADIUS
        live = (top > -STAMP) & (top < ROWS)
        tile = jnp.floor((whole_part[5:6] + RADIUS) * (1.0 / LANES))
        tile = jnp.where(live, tile, -1.0)
        same = tile_ids == jnp.broadcast_to(tile, (tiles, LANES))
        sorted_in[tiles * d : tiles * (d + 1), :] = jnp.where(same, 1.0, 0.0).astype(BF)

    upper = lax.broadcasted_iota(jnp.int32, (LANES, LANES), 0) <= lax.broadcasted_iota(
        jnp.int32, (LANES, LANES), 1
    )
    lower = lax.broadcasted_iota(jnp.int32, (tiles, tiles), 0) > lax.broadcasted_iota(
        jnp.int32, (tiles, tiles), 1
    )
    sums = jnp.concatenate(
        [jnp.where(upper, 1.0, 0.0).astype(BF), jnp.ones((LANES, LANES), BF)], axis=1
    )
    ranks = dot_nn(sorted_in[...], sums)
    before = jnp.zeros((tiles, LANES), F32)
    orders = []
    for d in range(cells):
        mine = slice(tiles * d, tiles * (d + 1))
        orders.append(ranks[mine, 0:LANES] + before)
        before = before + ranks[mine, LANES:]
    pairs = jnp.floor((before + 1.0) * 0.5)
    base = 2.0 * dot_nn(jnp.where(lower, 1.0, 0.0).astype(BF), pairs.astype(BF))
    for d in range(cells):
        mine = sorted_in[tiles * d : tiles * (d + 1), :].astype(F32)
        placed[d : d + 1, :] = jnp.sum(mine * (orders[d] + base), axis=0, keepdims=True) - 1.0
    total = (jnp.sum(pairs) * (2.0 / LANES)).astype(jnp.int32)

    slot = lax.broadcasted_iota(jnp.int32, (LANES, LANES), 0).astype(F32)
    eighth = lax.broadcasted_iota(jnp.int32, (32, coefs.shape[1]), 1) >> 3
    repeat = eighth == lax.broadcasted_iota(jnp.int32, eighth.shape, 0)
    repeat = jnp.where(repeat & (eighth < PIECES), 1.0, 0.0).astype(BF)

    def compact(q, carry):
        start = (q * LANES).astype(F32)
        for d in range(cells):
            match = placed[d : d + 1, :] - start == slot
            onehot[:, LANES * d : LANES * (d + 1)] = jnp.where(match, 1.0, 0.0).astype(BF)
        hot = onehot[...]
        got = dot_nt(flat[...], hot)
        coefs[pl.ds(pl.multiple_of(q * LANES, LANES), LANES), :] = lax.dot_general(
            got[0:32].astype(BF), repeat, (((0,), (0,)), ((), ())), preferred_element_type=F32
        )
        values = (
            got[PIECES : PIECES + 8] + got[PIECES + 8 : PIECES + 16] + got[PIECES + 16 : PIECES + 24]
        )
        valid = values[3:4] > 0.0
        spread = jnp.where(valid, values[3:4], 1.0)
        squared = spread * spread
        top_row = jnp.where(valid, (values[6:7] - me) * STAMP + values[4:5] + RADIUS, 0.0)
        column = jnp.where(valid, values[5:6] + RADIUS, 0.0)
        top_16 = jnp.floor(top_row * 0.0625) * 16.0
        tile = jnp.floor(column * (1.0 / LANES)) * LANES
        at = pl.ds(pl.multiple_of(q * 8, 8), 8)
        reals[at, :] = jnp.concatenate(
            [
                top_row - top_16 + values[1:2],
                values[2:3],
                (-0.5 / math.log(2.0)) / squared,
                jnp.where(valid, values[0:1], 0.0) / (2.0 * math.pi * squared),
                jnp.zeros((4, LANES), F32),
            ],
            axis=0,
        )
        whole[at, :] = jnp.concatenate(
            [
                top_16 + STAMP,
                top_row - top_16,
                tile,
                column - tile,
                jnp.zeros((4, LANES), F32),
            ],
            axis=0,
        ).astype(jnp.int32)
        return carry

    lax.fori_loop(0, (total + LANES - 1) // LANES, compact, 0)
    copy_r = pltpu.make_async_copy(reals, reals_s, sems.at[0])
    copy_w = pltpu.make_async_copy(whole, whole_s, sems.at[1])
    copy_r.start()
    copy_w.start()

    sub_i = lax.broadcasted_iota(jnp.int32, (8, LANES), 0)
    lane_i = lax.broadcasted_iota(jnp.int32, (8, LANES), 1)
    down = (sub_i - lane_i).astype(F32)
    diagonal = jnp.where((lane_i & 7) == sub_i, 1.0, 0.0)
    diagonal = jnp.concatenate([diagonal] * (coefs.shape[1] // LANES), axis=1)

    def group(g, carry):
        rows = coefs[pl.ds(pl.multiple_of(g * GROUP, GROUP), GROUP), :]
        spread = [
            jnp.broadcast_to(rows[i : i + 1, :], (8, rows.shape[1])) * diagonal
            for i in range(GROUP)
        ]
        pixels = dot_nn(jnp.concatenate(spread, axis=0).astype(BF), stack[...])
        for i in range(GROUP):
            image = [
                pixels[8 * i : 8 * i + 8, LANES * jb : LANES * (jb + 1)] for jb in range(STAMP // 8)
            ]
            images[g * GROUP + i] = jnp.concatenate(image, axis=0).astype(BF)
        return carry

    lax.fori_loop(0, (total + GROUP - 1) // GROUP, group, 0)

    copy_r.wait()
    copy_w.wait()

    def params(s):
        p = s * UNROLL
        return (p >> 7) << 3, p & (LANES - 1), p

    def toeplitz(base, shift, sharp, factor):
        halves = []
        for start in (-float(LANES), 0.0):
            pieces = []
            for row in (0.0, 8.0):
                far = base + (start - row)
                far = far - shift
                value = jnp.exp2(far * far * sharp)
                pieces.append(value if factor is None else value * factor)
            halves.append(jnp.concatenate(pieces, axis=0).astype(BF))
        return halves

    def make_rows(s, pair):
        r, c, _ = params(s)
        for v in (pair, pair + 1):
            shift = reals_s[r, c + v]
            sharp = reals_s[r + 2, c + v]
            edge = whole_s[r + 1, c + v]
            before, after = toeplitz(across_16, -shift, sharp, None)
            lanes = slice(LANES * (v % 2), LANES * (v % 2 + 1))
            row_16 = pl.multiple_of(whole_s[r, c + v], 16)
            for t in range((ROWS + 8) // 16):
                by_rows[v // 2, STAMP + 16 * t : STAMP + 16 * t + 16, lanes] = zero_16
            strip = by_rows.at[v // 2, pl.ds(row_16, ROWS + 8), lanes]
            for t in range(STAMP // 16 + 1):
                if t == 0:
                    rows_16 = jnp.where(sub_16 >= edge, after, zero_16)
                elif t == STAMP // 16:
                    rows_16 = jnp.where(sub_16 < edge, before, zero_16)
                else:
                    both = jnp.where(lane_16 < LANES - 16 * t, after, before)
                    rows_16 = pltpu.roll(both, 16 * t, 1)
                strip[16 * t : 16 * t + 16, :] = rows_16

    def make_columns(s, pair):
        r, c, _ = params(s)
        for v in (pair, pair + 1):
            shift = reals_s[r + 1, c + v]
            sharp = reals_s[r + 2, c + v]
            scale = reals_s[r + 3, c + v]
            turn = whole_s[r + 3, c + v]
            before, after = toeplitz(across_16, shift, sharp, scale)
            mine = lane_16 >= turn
            first = LANES * (v % 2)
            for t in range(STAMP // 16):
                both = after if t == 0 else jnp.where(lane_16 < LANES - 16 * t, after, before)
                both = pltpu.roll(both, (turn + 16 * t) & (LANES - 1), 1)
                by_columns[v // 2, first + 16 * t : first + 16 * t + 16, 0:LANES] = jnp.where(mine, both, zero_16)
                by_columns[v // 2, first + 16 * t : first + 16 * t + 16, LANES:] = jnp.where(mine, zero_16, both)

    across_16 = (lane_i - sub_i).astype(F32)
    lane_16 = lax.broadcasted_iota(jnp.int32, (16, LANES), 1)
    sub_16 = lax.broadcasted_iota(jnp.int32, (16, LANES), 0)
    zero_16 = jnp.zeros((16, LANES), BF)
    nothing = jnp.zeros((LANES, LANES), BF)

    def blocks(a, b):
        return jnp.concatenate(
            [jnp.concatenate([a, nothing], axis=1), jnp.concatenate([nothing, b], axis=1)], axis=0
        )

    def blur(s, w):
        _, _, p = params(s)
        pair = blocks(images[p + w], images[p + w + 1])
        blurred[w // 2] = dot_nn(
            by_rows[w // 2, STAMP : STAMP + ROWS + 8, :], pair
        ).astype(BF)

    def place(s, w):
        r, c, _ = params(s)
        lane_0 = pl.multiple_of(whole_s[r + 2, c + w], LANES)
        stamp = dot_nn(blurred[w // 2], by_columns[w // 2])
        window = canvas.at[:, pl.ds(lane_0, 2 * LANES)]
        window[...] = window[...] + stamp[0:ROWS]

    turns = jnp.maximum((total + UNROLL - 1) // UNROLL, 2)

    @pl.when(total > 0)
    def _():
        for w in range(0, UNROLL, 2):
            make_rows(0, w)
        for w in range(0, UNROLL, 2):
            blur(0, w)
            make_columns(0, w)
            make_rows(1, w)

        def step(s, carry):
            place(s - 2, 0)
            blur(s - 1, 0)
            for w in range(0, UNROLL, 2):
                if w + 2 < UNROLL:
                    place(s - 2, w + 2)
                    blur(s - 1, w + 2)
                make_columns(s - 1, w)
                make_rows(s, w)
            return carry

        lax.fori_loop(2, turns, step, 0)
        for w in range(0, UNROLL, 2):
            place(turns - 2, w)
            blur(turns - 1, w)
            make_columns(turns - 1, w)
        for w in range(0, UNROLL, 2):
            place(turns - 1, w)

    @pl.when(position == 0)
    def _():
        head = canvas[0:8, :]
        keep = lax.broadcasted_iota(jnp.int32, head.shape, 0) >= RADIUS
        canvas[0:8, :] = jnp.where(keep, head, 0.0)

    @pl.when(position == cells - 1)
    def _():
        tail = canvas[ROWS - 8 : ROWS, :]
        keep = lax.broadcasted_iota(jnp.int32, tail.shape, 0) < RADIUS
        canvas[ROWS - 8 : ROWS, :] = jnp.where(keep, tail, 0.0)

    columns = result.shape[1]
    spans = columns // SPAN
    copies = []
    for x in range(spans + 1):
        if x < spans:
            stop = columns + LANES if x == spans - 1 else (x + 1) * SPAN
            plane = canvas[:, x * SPAN : stop].astype(BF)
            smooth[:, x * SPAN : stop] = dot_nn(down_band[...], plane).astype(BF)
        if x > 0:
            starts = range((x - 1) * SPAN, x * SPAN, LANES)
            tall = jnp.concatenate([smooth[:, y : y + 2 * LANES] for y in starts], axis=0)
            tall = dot_nn(tall, side_band[...])
            for i, y in enumerate(starts):
                result[:, y : y + LANES] = tall[STAMP * i : STAMP * (i + 1)]
            ready = slice((x - 1) * SPAN, x * SPAN)
            copy = pltpu.make_async_copy(
                result.at[:, ready], out.at[:, ready], sems.at[1 + x]
            )
            copy.start()
            copies.append(copy)
    for copy in copies:
        copy.wait()


def gather_all(table, prepared):
    count = lax.axis_size("row")
    if count & (count - 1):
        return lax.all_gather(table, "row", tiled=True), prepared
    rounds = [(2, 4, 6)] if count > 4 else [(bit,) for bit in (2,) if bit < count]
    rounds += [(1 << b,) for b in range(3, count.bit_length() - 1)] + [(1,)] * (count > 1)
    for masks in rounds:
        others = [
            lax.ppermute(table, "row", [(i, i ^ mask) for i in range(count)]) for mask in masks
        ]
        table = jnp.concatenate([table] + others, axis=0)
        if masks is rounds[0]:
            table, prepared = lax.optimization_barrier((table, prepared))
    return table, prepared


def on_device(
    brightness,
    subpixel,
    profile_width,
    psf_coef,
    row_offset,
    column_offset,
    send_list,
    send_count,
    psf_basis,
    vertical_kernel,
    horizontal_kernel,
    columns,
):
    cells = lax.axis_size("row")
    cap = send_list.shape[2]
    vmem = pl.BlockSpec(memory_space=pltpu.VMEM)
    smem = pl.BlockSpec(memory_space=pltpu.SMEM)
    table = pl.pallas_call(
        pack_kernel,
        out_shape=pltpu.VMEM((TABLE, LANES), BF),
        in_specs=[vmem] * 8,
        out_specs=vmem,
        scratch_shapes=[pltpu.VMEM((TABLE, LANES), F32)],
        name="pack",
    )(
        brightness[None],
        subpixel,
        profile_width[None],
        psf_coef,
        row_offset[None],
        column_offset[None],
        jnp.transpose(send_list, (2, 0, 1)),
        send_count,
    )
    prepared = pl.pallas_call(
        prepare_kernel,
        out_shape=(
            pltpu.VMEM((8 * 32, STAMP * STAMP // 8), BF),
            pltpu.VMEM((STAMP, ROWS), BF),
            pltpu.VMEM((2 * LANES, LANES), BF),
            pltpu.VMEM((ROWS, columns + LANES), F32),
        ),
        in_specs=[smem, smem, vmem],
        out_specs=(vmem, vmem, vmem, vmem),
        cost_estimate=pl.CostEstimate(flops=0, bytes_accessed=2000000, transcendentals=0),
        name="prepare",
    )(vertical_kernel, horizontal_kernel, psf_basis)
    table, prepared = gather_all(table, prepared)
    most = cells * min(3 * cap, brightness.shape[0]) + columns // LANES
    chunks = -(-most // LANES)
    breadth = columns + LANES
    kernel = pl.pallas_call(
        render_kernel,
        out_shape=(
            jax.ShapeDtypeStruct((STAMP, columns), F32),
            pltpu.VMEM((ROWS, columns + LANES), F32),
        ),
        in_specs=[vmem] * 5,
        out_specs=(pl.BlockSpec(memory_space=pl.ANY), vmem),
        input_output_aliases={4: 1},
        scratch_shapes=[
            pltpu.VMEM(((chunks + 1) * LANES, STAMP, STAMP), BF),
            pltpu.VMEM((TABLE, cells * LANES), BF),
            pltpu.VMEM((cells, LANES), F32),
            pltpu.VMEM((cells * columns // LANES, LANES), BF),
            pltpu.VMEM((LANES, cells * LANES), BF),
            pltpu.VMEM((UNROLL // 2, 2 * STAMP + ROWS + 8, 2 * LANES), BF),
            pltpu.VMEM((UNROLL // 2, ROWS + 8, 2 * LANES), BF),
            pltpu.VMEM((UNROLL // 2, 2 * LANES, 2 * LANES), BF),
            pltpu.VMEM((chunks * LANES, 8 * 32), F32),
            pltpu.VMEM((chunks * 8 + 8, LANES), F32),
            pltpu.VMEM((chunks * 8 + 8, LANES), jnp.int32),
            pltpu.SMEM((chunks * 8 + 8, LANES), F32),
            pltpu.SMEM((chunks * 8 + 8, LANES), jnp.int32),
            pltpu.VMEM((STAMP, breadth), BF),
            pltpu.VMEM((STAMP, columns), F32),
            pltpu.SemaphoreType.DMA((2 + columns // SPAN,)),
        ],
        compiler_params=pltpu.CompilerParams(vmem_limit_bytes=44 * 1024 * 1024),
        name="render",
    )
    return kernel(table, *prepared)[0]


def solution(mesh):
    in_specs = (
        P(("exp", "row")),
        P(None, ("exp", "row")),
        P(("exp", "row")),
        P(None, ("exp", "row")),
        P(("exp", "row")),
        P(("exp", "row")),
        P(("exp", "row"), None, None),
        P(("exp", "row"), None),
        P(),
        P(),
        P(),
    )
    return jax.shard_map(
        functools.partial(on_device, columns=4096),
        mesh=mesh,
        in_specs=in_specs,
        out_specs=P(("exp", "row"), None),
        check_vma=False,
    )
```

```python
import functools
import math

import jax
import jax.numpy as jnp
from jax import lax
from jax.experimental import pallas as pl
from jax.experimental.pallas import tpu as pltpu
from jax.sharding import PartitionSpec as P

STAMP = 128
RADIUS = 4
LANES = 128
ROWS = STAMP + 2 * RADIUS
TABLE = 48
PIECES = 24
DEAD = -8.0
GROUP = 64
UNROLL = 16
SPAN = 1024
BF = jnp.bfloat16
F32 = jnp.float32


def dot_nt(a, b):
    return lax.dot_general(a, b, (((1,), (1,)), ((), ())), preferred_element_type=F32)


def dot_nn(a, b):
    return jnp.dot(a, b, preferred_element_type=F32)


def pack_kernel(bright, sub, width, coef, row, col, slots, counts, out, work):
    cap, _, cells = slots.shape
    objects = bright.shape[1]
    terms = coef.shape[0]
    eye = lax.broadcasted_iota(jnp.int32, (cells, cells), 0) == lax.broadcasted_iota(
        jnp.int32, (cells, cells), 1
    )
    limit = jnp.sum(jnp.where(eye, counts[...].astype(F32), 0.0), axis=1, keepdims=True)
    lane = lax.broadcasted_iota(jnp.int32, (cells, LANES), 1).astype(F32)
    block = lax.broadcasted_iota(jnp.int32, (cells, LANES), 0).astype(F32) - DEAD
    hits = jnp.zeros((cells, LANES), F32)
    for c in range(cap):
        entry = jnp.sum(jnp.where(eye, slots[c].astype(F32), 0.0), axis=1, keepdims=True)
        hit = (entry == lane) & (c < limit)
        hits = hits + jnp.where(hit, block, 0.0)
    target = jnp.sum(hits, axis=0, keepdims=True) + DEAD
    work[...] = jnp.zeros_like(work)
    work[0:terms, 0:objects] = coef[...].astype(F32)
    work[PIECES : PIECES + 1, 0:objects] = bright[...]
    work[PIECES + 1 : PIECES + 3, 0:objects] = sub[...]
    work[PIECES + 3 : PIECES + 4, 0:objects] = width[...]
    work[PIECES + 4 : PIECES + 5, 0:objects] = row[...].astype(F32)
    work[PIECES + 5 : PIECES + 6, 0:objects] = col[...].astype(F32)
    work[PIECES + 6 : PIECES + 7, :] = target
    full = work[PIECES : PIECES + 8, :]
    first = full.astype(BF).astype(F32)
    second = (full - first).astype(BF).astype(F32)
    work[PIECES : PIECES + 8, :] = first
    work[PIECES + 8 : PIECES + 16, :] = second
    work[PIECES + 16 : PIECES + 24, :] = full - first - second
    out[...] = work[...].astype(BF)


def band(weights, shape, flip):
    a = lax.broadcasted_iota(jnp.int32, shape, 0)
    b = lax.broadcasted_iota(jnp.int32, shape, 1)
    gap = a - b if flip else b - a
    total = jnp.zeros(shape, F32)
    for m in range(2 * RADIUS + 1):
        total = jnp.where(gap == m, weights[m], total)
    return total.astype(BF)


def prepare_kernel(vertical, horizontal, basis, stack, down_band, side_band, plane):
    terms = basis.shape[0]
    plane[...] = jnp.zeros_like(plane)
    down_band[...] = band(vertical, down_band.shape, False)
    side_band[...] = band(horizontal, side_band.shape, True)
    for k in range(0, stack.shape[0] // 8, 2):
        if k >= terms:
            stack[8 * k : 8 * k + 16, :] = jnp.zeros((16, stack.shape[1]), BF)
            continue
        even = basis[k].astype(F32)
        odd = basis[k + 1].astype(F32) if k + 1 < terms else jnp.zeros_like(even)
        for jb in range(STAMP // 8):
            both = jnp.concatenate(
                [even[8 * jb : 8 * jb + 8], odd[8 * jb : 8 * jb + 8]], axis=0
            )
            stack[8 * k : 8 * k + 16, LANES * jb : LANES * (jb + 1)] = both.astype(BF)


def render_kernel(
    table,
    stack,
    down_band,
    side_band,
    plane,
    out,
    canvas,
    images,
    flat,
    placed,
    sorted_in,
    onehot,
    by_rows,
    blurred,
    by_columns,
    coefs,
    reals,
    whole,
    reals_s,
    whole_s,
    smooth,
    result,
    sems,
):
    cells = table.shape[0] // TABLE
    position = lax.axis_index("row")
    me = position.astype(F32)
    tiles = canvas.shape[1] // LANES - 1

    tile_ids = lax.broadcasted_iota(jnp.int32, (tiles, LANES), 0).astype(F32)
    for d in range(cells):
        part = table[TABLE * d : TABLE * (d + 1), :]
        lanes = slice(LANES * d, LANES * (d + 1))
        flat[:, lanes] = part
        part = part.astype(F32)
        whole_part = (
            part[PIECES : PIECES + 8] + part[PIECES + 8 : PIECES + 16] + part[PIECES + 16 : TABLE]
        )
        top = (whole_part[6:7] - me) * STAMP + whole_part[4:5] + RADIUS
        live = (top > -STAMP) & (top < ROWS)
        tile = jnp.floor((whole_part[5:6] + RADIUS) * (1.0 / LANES))
        tile = jnp.where(live, tile, -1.0)
        same = tile_ids == jnp.broadcast_to(tile, (tiles, LANES))
        sorted_in[tiles * d : tiles * (d + 1), :] = jnp.where(same, 1.0, 0.0).astype(BF)

    upper = lax.broadcasted_iota(jnp.int32, (LANES, LANES), 0) <= lax.broadcasted_iota(
        jnp.int32, (LANES, LANES), 1
    )
    lower = lax.broadcasted_iota(jnp.int32, (tiles, tiles), 0) > lax.broadcasted_iota(
        jnp.int32, (tiles, tiles), 1
    )
    sums = jnp.concatenate(
        [jnp.where(upper, 1.0, 0.0).astype(BF), jnp.ones((LANES, LANES), BF)], axis=1
    )
    ranks = dot_nn(sorted_in[...], sums)
    before = jnp.zeros((tiles, LANES), F32)
    orders = []
    for d in range(cells):
        mine = slice(tiles * d, tiles * (d + 1))
        orders.append(ranks[mine, 0:LANES] + before)
        before = before + ranks[mine, LANES:]
    pairs = jnp.floor((before + 1.0) * 0.5)
    base = 2.0 * dot_nn(jnp.where(lower, 1.0, 0.0).astype(BF), pairs.astype(BF))
    for d in range(cells):
        mine = sorted_in[tiles * d : tiles * (d + 1), :].astype(F32)
        placed[d : d + 1, :] = jnp.sum(mine * (orders[d] + base), axis=0, keepdims=True) - 1.0
    total = (jnp.sum(pairs) * (2.0 / LANES)).astype(jnp.int32)

    slot = lax.broadcasted_iota(jnp.int32, (LANES, LANES), 0).astype(F32)
    eighth = lax.broadcasted_iota(jnp.int32, (32, coefs.shape[1]), 1) >> 3
    repeat = eighth == lax.broadcasted_iota(jnp.int32, eighth.shape, 0)
    repeat = jnp.where(repeat & (eighth < PIECES), 1.0, 0.0).astype(BF)

    def compact(q, carry):
        start = (q * LANES).astype(F32)
        for d in range(cells):
            match = placed[d : d + 1, :] - start == slot
            onehot[:, LANES * d : LANES * (d + 1)] = jnp.where(match, 1.0, 0.0).astype(BF)
        hot = onehot[...]
        got = dot_nt(flat[...], hot)
        coefs[pl.ds(pl.multiple_of(q * LANES, LANES), LANES), :] = lax.dot_general(
            got[0:32].astype(BF), repeat, (((0,), (0,)), ((), ())), preferred_element_type=F32
        )
        values = (
            got[PIECES : PIECES + 8] + got[PIECES + 8 : PIECES + 16] + got[PIECES + 16 : PIECES + 24]
        )
        valid = values[3:4] > 0.0
        spread = jnp.where(valid, values[3:4], 1.0)
        squared = spread * spread
        top_row = jnp.where(valid, (values[6:7] - me) * STAMP + values[4:5] + RADIUS, 0.0)
        column = jnp.where(valid, values[5:6] + RADIUS, 0.0)
        top_16 = jnp.floor(top_row * 0.0625) * 16.0
        tile = jnp.floor(column * (1.0 / LANES)) * LANES
        at = pl.ds(pl.multiple_of(q * 8, 8), 8)
        reals[at, :] = jnp.concatenate(
            [
                top_row - top_16 + values[1:2],
                values[2:3],
                (-0.5 / math.log(2.0)) / squared,
                jnp.where(valid, values[0:1], 0.0) / (2.0 * math.pi * squared),
                jnp.zeros((4, LANES), F32),
            ],
            axis=0,
        )
        whole[at, :] = jnp.concatenate(
            [
                top_16 + STAMP,
                top_row - top_16,
                tile,
                column - tile,
                jnp.zeros((4, LANES), F32),
            ],
            axis=0,
        ).astype(jnp.int32)
        return carry

    lax.fori_loop(0, (total + LANES - 1) // LANES, compact, 0)
    copy_r = pltpu.make_async_copy(reals, reals_s, sems.at[0])
    copy_w = pltpu.make_async_copy(whole, whole_s, sems.at[1])
    copy_r.start()
    copy_w.start()

    sub_i = lax.broadcasted_iota(jnp.int32, (8, LANES), 0)
    lane_i = lax.broadcasted_iota(jnp.int32, (8, LANES), 1)
    down = (sub_i - lane_i).astype(F32)
    diagonal = jnp.where((lane_i & 7) == sub_i, 1.0, 0.0)
    diagonal = jnp.concatenate([diagonal] * (coefs.shape[1] // LANES), axis=1)

    def group(g, carry):
        rows = coefs[pl.ds(pl.multiple_of(g * GROUP, GROUP), GROUP), :]
        spread = [
            jnp.broadcast_to(rows[i : i + 1, :], (8, rows.shape[1])) * diagonal
            for i in range(GROUP)
        ]
        pixels = dot_nn(jnp.concatenate(spread, axis=0).astype(BF), stack[...])
        for i in range(GROUP):
            image = [
                pixels[8 * i : 8 * i + 8, LANES * jb : LANES * (jb + 1)] for jb in range(STAMP // 8)
            ]
            images[g * GROUP + i] = jnp.concatenate(image, axis=0).astype(BF)
        return carry

    lax.fori_loop(0, (total + GROUP - 1) // GROUP, group, 0)

    copy_r.wait()
    copy_w.wait()

    def params(s):
        p = s * UNROLL
        return (p >> 7) << 3, p & (LANES - 1), p

    def toeplitz(base, shift, sharp, factor):
        halves = []
        for start in (-float(LANES), 0.0):
            pieces = []
            for row in (0.0, 8.0):
                far = base + (start - row)
                far = far - shift
                value = jnp.exp2(far * far * sharp)
                pieces.append(value if factor is None else value * factor)
            halves.append(jnp.concatenate(pieces, axis=0).astype(BF))
        return halves

    def make_rows(s, pair):
        r, c, _ = params(s)
        for v in (pair, pair + 1):
            shift = reals_s[r, c + v]
            sharp = reals_s[r + 2, c + v]
            edge = whole_s[r + 1, c + v]
            before, after = toeplitz(across_16, -shift, sharp, None)
            lanes = slice(LANES * (v % 2), LANES * (v % 2 + 1))
            row_16 = pl.multiple_of(whole_s[r, c + v], 16)
            for t in range((ROWS + 8) // 16):
                by_rows[v // 2, STAMP + 16 * t : STAMP + 16 * t + 16, lanes] = zero_16
            strip = by_rows.at[v // 2, pl.ds(row_16, ROWS + 8), lanes]
            for t in range(STAMP // 16 + 1):
                if t == 0:
                    rows_16 = jnp.where(sub_16 >= edge, after, zero_16)
                elif t == STAMP // 16:
                    rows_16 = jnp.where(sub_16 < edge, before, zero_16)
                else:
                    both = jnp.where(lane_16 < LANES - 16 * t, after, before)
                    rows_16 = pltpu.roll(both, 16 * t, 1)
                strip[16 * t : 16 * t + 16, :] = rows_16

    def make_columns(s, pair):
        r, c, _ = params(s)
        for v in (pair, pair + 1):
            shift = reals_s[r + 1, c + v]
            sharp = reals_s[r + 2, c + v]
            scale = reals_s[r + 3, c + v]
            turn = whole_s[r + 3, c + v]
            before, after = toeplitz(across_16, shift, sharp, scale)
            mine = lane_16 >= turn
            first = LANES * (v % 2)
            for t in range(STAMP // 16):
                both = after if t == 0 else jnp.where(lane_16 < LANES - 16 * t, after, before)
                both = pltpu.roll(both, (turn + 16 * t) & (LANES - 1), 1)
                by_columns[v // 2, first + 16 * t : first + 16 * t + 16, 0:LANES] = jnp.where(mine, both, zero_16)
                by_columns[v // 2, first + 16 * t : first + 16 * t + 16, LANES:] = jnp.where(mine, zero_16, both)

    across_16 = (lane_i - sub_i).astype(F32)
    lane_16 = lax.broadcasted_iota(jnp.int32, (16, LANES), 1)
    sub_16 = lax.broadcasted_iota(jnp.int32, (16, LANES), 0)
    zero_16 = jnp.zeros((16, LANES), BF)
    nothing = jnp.zeros((LANES, LANES), BF)

    def blocks(a, b):
        return jnp.concatenate(
            [jnp.concatenate([a, nothing], axis=1), jnp.concatenate([nothing, b], axis=1)], axis=0
        )

    def blur(s, w):
        _, _, p = params(s)
        pair = blocks(images[p + w], images[p + w + 1])
        blurred[w // 2] = dot_nn(
            by_rows[w // 2, STAMP : STAMP + ROWS + 8, :], pair
        ).astype(BF)

    def place(s, w):
        r, c, _ = params(s)
        lane_0 = pl.multiple_of(whole_s[r + 2, c + w], LANES)
        stamp = dot_nn(blurred[w // 2], by_columns[w // 2])
        window = canvas.at[:, pl.ds(lane_0, 2 * LANES)]
        window[...] = window[...] + stamp[0:ROWS]

    turns = jnp.maximum((total + UNROLL - 1) // UNROLL, 2)

    @pl.when(total > 0)
    def _():
        for w in range(0, UNROLL, 2):
            make_rows(0, w)
        for w in range(0, UNROLL, 2):
            blur(0, w)
            make_columns(0, w)
            make_rows(1, w)

        def step(s, carry):
            place(s - 2, 0)
            blur(s - 1, 0)
            for w in range(0, UNROLL, 2):
                if w + 2 < UNROLL:
                    place(s - 2, w + 2)
                    blur(s - 1, w + 2)
                make_columns(s - 1, w)
                make_rows(s, w)
            return carry

        lax.fori_loop(2, turns, step, 0)
        for w in range(0, UNROLL, 2):
            place(turns - 2, w)
            blur(turns - 1, w)
            make_columns(turns - 1, w)
        for w in range(0, UNROLL, 2):
            place(turns - 1, w)

    @pl.when(position == 0)
    def _():
        head = canvas[0:8, :]
        keep = lax.broadcasted_iota(jnp.int32, head.shape, 0) >= RADIUS
        canvas[0:8, :] = jnp.where(keep, head, 0.0)

    @pl.when(position == cells - 1)
    def _():
        tail = canvas[ROWS - 8 : ROWS, :]
        keep = lax.broadcasted_iota(jnp.int32, tail.shape, 0) < RADIUS
        canvas[ROWS - 8 : ROWS, :] = jnp.where(keep, tail, 0.0)

    columns = result.shape[1]
    spans = columns // SPAN
    copies = []
    for x in range(spans + 1):
        if x < spans:
            stop = columns + LANES if x == spans - 1 else (x + 1) * SPAN
            plane = canvas[:, x * SPAN : stop].astype(BF)
            smooth[:, x * SPAN : stop] = dot_nn(down_band[...], plane).astype(BF)
        if x > 0:
            starts = range((x - 1) * SPAN, x * SPAN, LANES)
            tall = jnp.concatenate([smooth[:, y : y + 2 * LANES] for y in starts], axis=0)
            tall = dot_nn(tall, side_band[...])
            for i, y in enumerate(starts):
                result[:, y : y + LANES] = tall[STAMP * i : STAMP * (i + 1)]
            ready = slice((x - 1) * SPAN, x * SPAN)
            copy = pltpu.make_async_copy(
                result.at[:, ready], out.at[:, ready], sems.at[1 + x]
            )
            copy.start()
            copies.append(copy)
    for copy in copies:
        copy.wait()


def gather_all(table, prepared):
    count = lax.axis_size("row")
    if count & (count - 1):
        return lax.all_gather(table, "row", tiled=True), prepared
    rounds = [(2, 4, 6)] if count > 4 else [(bit,) for bit in (2,) if bit < count]
    rounds += [(1 << b,) for b in range(3, count.bit_length() - 1)] + [(1,)] * (count > 1)
    for masks in rounds:
        others = [
            lax.ppermute(table, "row", [(i, i ^ mask) for i in range(count)]) for mask in masks
        ]
        table = jnp.concatenate([table] + others, axis=0)
        if masks is rounds[0]:
            table, prepared = lax.optimization_barrier((table, prepared))
    return table, prepared


def on_device(
    brightness,
    subpixel,
    profile_width,
    psf_coef,
    row_offset,
    column_offset,
    send_list,
    send_count,
    psf_basis,
    vertical_kernel,
    horizontal_kernel,
    columns,
):
    cells = lax.axis_size("row")
    cap = send_list.shape[2]
    vmem = pl.BlockSpec(memory_space=pltpu.VMEM)
    smem = pl.BlockSpec(memory_space=pltpu.SMEM)
    table = pl.pallas_call(
        pack_kernel,
        out_shape=pltpu.VMEM((TABLE, LANES), BF),
        in_specs=[vmem] * 8,
        out_specs=vmem,
        scratch_shapes=[pltpu.VMEM((TABLE, LANES), F32)],
        name="pack",
    )(
        brightness[None],
        subpixel,
        profile_width[None],
        psf_coef,
        row_offset[None],
        column_offset[None],
        jnp.transpose(send_list, (2, 0, 1)),
        send_count,
    )
    prepared = pl.pallas_call(
        prepare_kernel,
        out_shape=(
            pltpu.VMEM((8 * 32, STAMP * STAMP // 8), BF),
            pltpu.VMEM((STAMP, ROWS), BF),
            pltpu.VMEM((2 * LANES, LANES), BF),
            pltpu.VMEM((ROWS, columns + LANES), F32),
        ),
        in_specs=[smem, smem, vmem],
        out_specs=(vmem, vmem, vmem, vmem),
        cost_estimate=pl.CostEstimate(flops=0, bytes_accessed=2000000, transcendentals=0),
        name="prepare",
    )(vertical_kernel, horizontal_kernel, psf_basis)
    table, prepared = gather_all(table, prepared)
    most = cells * min(3 * cap, brightness.shape[0]) + columns // LANES
    chunks = -(-most // LANES)
    breadth = columns + LANES
    kernel = pl.pallas_call(
        render_kernel,
        out_shape=(
            jax.ShapeDtypeStruct((STAMP, columns), F32),
            pltpu.VMEM((ROWS, columns + LANES), F32),
        ),
        in_specs=[vmem] * 5,
        out_specs=(pl.BlockSpec(memory_space=pl.ANY), vmem),
        input_output_aliases={4: 1},
        scratch_shapes=[
            pltpu.VMEM(((chunks + 1) * LANES, STAMP, STAMP), BF),
            pltpu.VMEM((TABLE, cells * LANES), BF),
            pltpu.VMEM((cells, LANES), F32),
            pltpu.VMEM((cells * columns // LANES, LANES), BF),
            pltpu.VMEM((LANES, cells * LANES), BF),
            pltpu.VMEM((UNROLL // 2, 2 * STAMP + ROWS + 8, 2 * LANES), BF),
            pltpu.VMEM((UNROLL // 2, ROWS + 8, 2 * LANES), BF),
            pltpu.VMEM((UNROLL // 2, 2 * LANES, 2 * LANES), BF),
            pltpu.VMEM((chunks * LANES, 8 * 32), F32),
            pltpu.VMEM((chunks * 8 + 8, LANES), F32),
            pltpu.VMEM((chunks * 8 + 8, LANES), jnp.int32),
            pltpu.SMEM((chunks * 8 + 8, LANES), F32),
            pltpu.SMEM((chunks * 8 + 8, LANES), jnp.int32),
            pltpu.VMEM((STAMP, breadth), BF),
            pltpu.VMEM((STAMP, columns), F32),
            pltpu.SemaphoreType.DMA((2 + columns // SPAN,)),
        ],
        compiler_params=pltpu.CompilerParams(vmem_limit_bytes=44 * 1024 * 1024),
        name="render",
    )
    return kernel(table, *prepared)[0]


def solution(mesh):
    in_specs = (
        P(("exp", "row")),
        P(None, ("exp", "row")),
        P(("exp", "row")),
        P(None, ("exp", "row")),
        P(("exp", "row")),
        P(("exp", "row")),
        P(("exp", "row"), None, None),
        P(("exp", "row"), None),
        P(),
        P(),
        P(),
    )
    return jax.shard_map(
        functools.partial(on_device, columns=4096),
        mesh=mesh,
        in_specs=in_specs,
        out_specs=P(("exp", "row"), None),
        check_vma=False,
    )
```
